32 devices in a mesh: ia: 4 (over y, x), ja: 4 (over z), ka: 2 (over core).
Axes of the slice: x: 2, y: 2, z: 4, core: 2. Of those that a mesh axis runs over, the one named last changes fastest.
Arguments:
- inputs: bfloat16 [4, 1024, 4096], P('ia', 'ja', 'ka'), may hold values from -0.09375 to 0.09375
- attn_out: bfloat16 [4, 1024, 4096], P(None, 'ja', ('ia', 'ka')), may hold values from -0.09375 to 0.09375
- grad_out: bfloat16 [4, 1024, 4096], P('ia', 'ja', 'ka'), may hold values from -6 to 6
- grad_query: bfloat16 [4, 1024, 4096], P(None, 'ja', ('ia', 'ka')), may hold values from -6 to 6
- grad_key: bfloat16 [4, 1024, 4096], P(None, 'ja', ('ia', 'ka')), may hold values from -6 to 6
- grad_value: bfloat16 [4, 1024, 4096], P(None, 'ja', ('ia', 'ka')), may hold values from -6 to 6
- query_weight: bfloat16 [4096, 4096], P('ka', ('ia', 'ja')), may hold values from -0.09375 to 0.09375
- key_weight: bfloat16 [4096, 4096], P('ka', ('ia', 'ja')), may hold values from -0.09375 to 0.09375
- value_weight: bfloat16 [4096, 4096], P('ka', ('ia', 'ja')), may hold values from -0.09375 to 0.09375
Outputs:
- grad_inputs: bfloat16 [4, 1024, 4096], P('ia', 'ja', 'ka')
- query_weight_grad: float32 [4096, 4096], P('ka', ('ia', 'ja'))
- key_weight_grad: float32 [4096, 4096], P('ka', ('ia', 'ja'))
- value_weight_grad: float32 [4096, 4096], P('ka', ('ia', 'ja'))
- output_weight_grad: float32 [4096, 4096], P(('ia', 'ja'), 'ka')
The draws below stay inside these ranges and needn't reach their ends.
All inputs are finite; a program needn't handle non-finite values.
Results may differ from the reference program's by a relative error of at most 0.015.
Values may be sent and summed in bfloat16 or wider, within the bound.
No kernel may reach another device: no remote copies, remote signals or barrier semaphores. Data moves between devices by JAX's collectives and lax.ppermute only.
A program may use at most 128 MiB of HBM per device.

```python
import jax
import jax.numpy as jnp

D = 4096
F = 4096
BANKS = 4
BANK_TOK = 1024
TOKENS = 4096


def level_of(key, extent, cuts, low, top_value):
    gain = 1.0
    for position, shards_of in cuts:
        heights = jax.random.uniform(jax.random.fold_in(jax.random.fold_in(key, 6), position), (shards_of,), jnp.float32, low / len(cuts), top_value / len(cuts))
        gain = gain * jnp.repeat(jnp.exp(heights), extent[position] // shards_of).reshape((-1,) + (1,) * (len(extent) - 1 - position))
    return gain


def gaussian(key, dims, deviation, bound, split=(), kind=jnp.bfloat16):
    values = jax.random.normal(key, dims, jnp.float32) * deviation
    if len(split) > 0:
        values = level_of(key, dims, split, -0.22, 0.18) * values
    return jnp.clip(values, min=-bound, max=bound).astype(kind)


def setup_inputs(seed: int = 0) -> dict:
    streams_of = jax.random.split(jax.random.key(seed), 10)
    return {
        "inputs": gaussian(streams_of[0], (BANKS, BANK_TOK, D), (TOKENS ** -0.5), 0.09375, ((0, 4), (1, 4), (2, 2))),
        "attn_out": gaussian(streams_of[1], (BANKS, BANK_TOK, F), (TOKENS ** -0.5), 0.09375, ((1, 4), (2, 8))),
        "grad_out": gaussian(streams_of[2], (BANKS, BANK_TOK, D), 1.0, 6.0, ((0, 4), (1, 4), (2, 2))),
        "grad_query": gaussian(streams_of[3], (BANKS, BANK_TOK, F), 1.0, 6.0, ((1, 4), (2, 8))),
        "grad_key": gaussian(streams_of[4], (BANKS, BANK_TOK, F), 1.0, 6.0, ((1, 4), (2, 8))),
        "grad_value": gaussian(streams_of[5], (BANKS, BANK_TOK, F), 1.0, 6.0, ((1, 4), (2, 8))),
        "query_weight": gaussian(streams_of[6], (D, F), D ** -0.5, 0.09375, ((0, 2), (1, 16))),
        "key_weight": gaussian(streams_of[7], (D, F), D ** -0.5, 0.09375, ((0, 2), (1, 16))),
        "value_weight": gaussian(streams_of[8], (D, F), D ** -0.5, 0.09375, ((0, 2), (1, 16))),
    }


def flatten_rows(array):
    return array.reshape(-1, array.shape[-1])


def reference(inputs, attn_out, grad_out, grad_query, grad_key, grad_value, query_weight, key_weight, value_weight):
    rows_in = flatten_rows(inputs)
    rows_attn = flatten_rows(attn_out)
    rows_grad = flatten_rows(grad_out)
    grad_q = flatten_rows(grad_query)
    grad_k = flatten_rows(grad_key)
    grad_v = flatten_rows(grad_value)
    summed = jnp.dot(grad_q, query_weight.T, preferred_element_type=jnp.float32)
    summed = summed + jnp.dot(grad_k, key_weight.T, preferred_element_type=jnp.float32)
    summed = summed + jnp.dot(grad_v, value_weight.T, preferred_element_type=jnp.float32)
    grad_inputs = summed.astype(jnp.bfloat16).reshape(inputs.shape)
    query_weight_grad = jnp.dot(rows_in.T, grad_q, preferred_element_type=jnp.float32)
    key_weight_grad = jnp.dot(rows_in.T, grad_k, preferred_element_type=jnp.float32)
    value_weight_grad = jnp.dot(rows_in.T, grad_v, preferred_element_type=jnp.float32)
    output_weight_grad = jnp.dot(rows_attn.T, rows_grad, preferred_element_type=jnp.float32)
    return (grad_inputs, query_weight_grad, key_weight_grad, value_weight_grad, output_weight_grad)
```

```python
import jax
import jax.numpy as jnp
from jax import lax
from jax.sharding import PartitionSpec as P

BF16 = jnp.bfloat16
F32 = jnp.float32


def ring_place(j, n):
    return jnp.where(j % 2 == 1, (j + 1) // 2, (n - j // 2) % n)


def ring_pairs(n):
    order = [0] + list(range(1, n, 2)) + list(range(n - 2, 0, -2))
    return [(order[p], order[(p + 1) % n]) for p in range(n)]


def dot_rows(a, b):
    return lax.dot_general(a, b, (((0,), (0,)), ((), ())), preferred_element_type=F32)


def dot_cols(a, b):
    return lax.dot_general(a, b, (((1,), (1,)), ((), ())), preferred_element_type=F32)


def build(mesh):
    ni, nj, nk = mesh.shape["ia"], mesh.shape["ja"], mesh.shape["ka"]
    assert ni == 4 and nj % nk == 0
    per = nj // nk
    swap_x = [(i, i ^ 1) for i in range(ni)]
    swap_y = [(i, i ^ 2) for i in range(ni)]
    ring = ring_pairs(nj)
    core_ring = [(k, (k + 1) % nk) for k in range(nk)]

    def deal_pairs(step, dy):
        pairs = []
        for i in range(ni):
            for j in range(nj):
                for k in range(nk):
                    to_j, to_k = per * k + (j + step) % per, j // per
                    pairs.append(
                        ((i * nj + j) * nk + k, ((i ^ (2 * dy)) * nj + to_j) * nk + to_k)
                    )
        return pairs

    def local(
        inputs,
        attn_out,
        grad_out,
        grad_query,
        grad_key,
        grad_value,
        query_weight,
        key_weight,
        value_weight,
    ):
        i, j, k = lax.axis_index("ia"), lax.axis_index("ja"), lax.axis_index("ka")
        tok, width = inputs.shape[1], inputs.shape[2]
        feat = grad_query.shape[2] // per
        place = ring_place(j, nj)
        grads = (grad_query, grad_key, grad_value)

        rows = inputs.reshape(tok, width)
        blocks = []
        for step in range(nj):
            blocks.append(rows)
            blocks.append(lax.ppermute(rows, "ia", swap_x))
            if step < nj - 1:
                rows = lax.ppermute(rows, "ja", ring)
        x_all = jnp.concatenate(blocks, axis=0)

        w_own = jnp.concatenate((query_weight, key_weight, value_weight), axis=1)
        w_both = jnp.concatenate((w_own, lax.ppermute(w_own, "ia", swap_y)), axis=1)

        go_own = grad_out.reshape(tok, width)
        go_pair = jnp.concatenate((go_own, lax.ppermute(go_own, "ia", swap_x)), axis=0)
        go_all = jnp.concatenate((go_pair, lax.ppermute(go_pair, "ia", swap_y)), axis=0)

        attn = jnp.concatenate(
            [lax.dynamic_index_in_dim(attn_out, i ^ r, 0, keepdims=False) for r in range(ni)], axis=0
        )
        attn_list = [attn]
        for _ in range(nk - 1):
            attn_list.append(lax.ppermute(attn_list[-1], "ka", core_ring))
        attn_all = jnp.stack(attn_list)

        g_all = jnp.zeros((nj, 2 * tok, 6 * feat), BF16)
        for dy in range(2):
            for step in range(per):
                chunk = (j + step) % per
                piece = jnp.concatenate(
                    [
                        jnp.concatenate(
                            [
                                lax.dynamic_slice(
                                    grad, (i ^ (2 * dy) ^ dx, 0, chunk * feat), (1, tok, feat)
                                ).reshape(tok, feat)
                                for grad in grads
                            ],
                            axis=1,
                        )
                        for dx in range(2)
                    ],
                    axis=0,
                )
                piece = lax.ppermute(piece, ("ia", "ja", "ka"), deal_pairs(step, dy))
                for hop in range(nk):
                    source = per * ((k - hop) % nk) + (j % per - step) % per
                    slot = (place - ring_place(source, nj)) % nj
                    g_all = lax.dynamic_update_slice(
                        g_all, piece[None], (slot, 0, dy * 3 * feat)
                    )
                    if hop < nk - 1:
                        piece = lax.ppermute(piece, "ka", core_ring)

        def output_chunk(step):
            back = (place - step) % nj
            dest = jnp.where(
                back == 0, 0, jnp.where(back <= nj // 2, 2 * back - 1, 2 * (nj - back))
            )
            part = lax.dynamic_slice(
                attn_all, ((k - dest // per) % nk, 0, (dest % per) * feat), (1, ni * tok, feat)
            )
            return dot_rows(part.reshape(ni * tok, feat), go_all)

        moving = output_chunk(1).astype(BF16)
        for step in range(1, nj):
            moving = lax.ppermute(moving, "ja", ring)
            total = output_chunk((step + 1) % nj) + moving.astype(F32)
            moving = total.astype(BF16)
        output_weight_grad = total

        def input_chunk(step):
            other = dot_cols(g_all[step % nj, tok:], w_both).astype(BF16)
            other = lax.ppermute(other, "ia", swap_x)
            return dot_cols(g_all[step % nj, :tok], w_both) + other.astype(F32)

        moving = input_chunk(1).astype(BF16)
        for step in range(1, nj):
            moving = lax.ppermute(moving, "ja", ring)
            moving = (input_chunk(step + 1) + moving.astype(F32)).astype(BF16)
        grad_inputs = moving.reshape(inputs.shape)

        g_flat = g_all.reshape(nj * 2 * tok, 6 * feat)
        weight_grads = []
        for w in range(3):
            other = dot_rows(x_all, g_flat[:, (3 + w) * feat : (4 + w) * feat]).astype(BF16)
            other = lax.ppermute(other, "ia", swap_y)
            weight_grads.append(
                dot_rows(x_all, g_flat[:, w * feat : (w + 1) * feat]) + other.astype(F32)
            )
        return (grad_inputs, *weight_grads, output_weight_grad)

    return local


def solution(mesh):
    return jax.shard_map(
        build(mesh),
        mesh=mesh,
        in_specs=(
            P("ia", "ja", "ka"),
            P(None, "ja", ("ia", "ka")),
            P("ia", "ja", "ka"),
            P(None, "ja", ("ia", "ka")),
            P(None, "ja", ("ia", "ka")),
            P(None, "ja", ("ia", "ka")),
            P("ka", ("ia", "ja")),
            P("ka", ("ia", "ja")),
            P("ka", ("ia", "ja")),
        ),
        out_specs=(
            P("ia", "ja", "ka"),
            P("ka", ("ia", "ja")),
            P("ka", ("ia", "ja")),
            P("ka", ("ia", "ja")),
            P(("ia", "ja"), "ka"),
        ),
        check_vma=False,
    )
```

```python
import jax
import jax.numpy as jnp
from jax import lax
from jax.sharding import PartitionSpec as P

BF16 = jnp.bfloat16
F32 = jnp.float32


def ring_place(j, n):
    return jnp.where(j % 2 == 1, (j + 1) // 2, (n - j // 2) % n)


def ring_pairs(n):
    order = [0] + list(range(1, n, 2)) + list(range(n - 2, 0, -2))
    return [(order[p], order[(p + 1) % n]) for p in range(n)]


def dot_rows(a, b):
    return lax.dot_general(a, b, (((0,), (0,)), ((), ())), preferred_element_type=F32)


def dot_cols(a, b):
    return lax.dot_general(a, b, (((1,), (1,)), ((), ())), preferred_element_type=F32)


def build(mesh):
    ni, nj, nk = mesh.shape["ia"], mesh.shape["ja"], mesh.shape["ka"]
    assert ni == 4 and nj % nk == 0
    per = nj // nk
    swap_x = [(i, i ^ 1) for i in range(ni)]
    swap_y = [(i, i ^ 2) for i in range(ni)]
    ring = ring_pairs(nj)
    core_ring = [(k, (k + 1) % nk) for k in range(nk)]

    def deal_pairs(step, dy):
        pairs = []
        for i in range(ni):
            for j in range(nj):
                for k in range(nk):
                    to_j, to_k = per * k + (j + step) % per, j // per
                    pairs.append(
                        ((i * nj + j) * nk + k, ((i ^ (2 * dy)) * nj + to_j) * nk + to_k)
                    )
        return pairs

    def local(
        inputs,
        attn_out,
        grad_out,
        grad_query,
        grad_key,
        grad_value,
        query_weight,
        key_weight,
        value_weight,
    ):
        i, j, k = lax.axis_index("ia"), lax.axis_index("ja"), lax.axis_index("ka")
        tok, width = inputs.shape[1], inputs.shape[2]
        feat = grad_query.shape[2] // per
        place = ring_place(j, nj)
        grads = (grad_query, grad_key, grad_value)

        def after(value, *earlier):
            return lax.optimization_barrier((value, *earlier))[0]

        go_own = grad_out.reshape(tok, width)
        go_pair = jnp.concatenate((go_own, lax.ppermute(go_own, "ia", swap_x)), axis=0)

        weights = (query_weight, key_weight, value_weight)
        others = [lax.ppermute(query_weight, "ia", swap_y)]
        go_all = jnp.concatenate((go_pair, lax.ppermute(go_pair, "ia", swap_y)), axis=0)
        others.append(lax.ppermute(after(key_weight, others[0]), "ia", swap_y))
        others.append(lax.ppermute(after(value_weight, go_all), "ia", swap_y))
        w_both = jnp.concatenate((*weights, *others), axis=1)

        attn = jnp.concatenate(
            [lax.dynamic_index_in_dim(attn_out, i ^ r, 0, keepdims=False) for r in range(ni)], axis=0
        )
        attn_list = [attn]
        for _ in range(nk - 1):
            attn_list.append(lax.ppermute(attn_list[-1], "ka", core_ring))
        attn_all = jnp.stack(attn_list)

        def deal_piece(step, dy):
            chunk = (j + step) % per
            return jnp.concatenate(
                [
                    jnp.concatenate(
                        [
                            lax.dynamic_slice(
                                grad, (i ^ (2 * dy) ^ dx, 0, chunk * feat), (1, tok, feat)
                            ).reshape(tok, feat)
                            for grad in grads
                        ],
                        axis=1,
                    )
                    for dx in range(2)
                ],
                axis=0,
            )

        deals = [(step, dy) for step in range(per) for dy in range(2)]
        rows = inputs.reshape(tok, width)
        blocks = [rows, lax.ppermute(after(rows, go_pair), "ia", swap_x)]
        dealt = []
        queue = [rows, rows]

        def send_deal():
            step, dy = deals[len(dealt)]
            piece = after(deal_piece(step, dy), queue[-2])
            dealt.append(lax.ppermute(piece, ("ia", "ja", "ka"), deal_pairs(step, dy)))
            queue.append(dealt[-1])

        for step in range(1, nj):
            rows = lax.ppermute(after(rows, queue[-2]), "ja", ring)
            queue.append(rows)
            blocks.append(rows)
            blocks.append(lax.ppermute(rows, "ia", swap_x))
            if len(dealt) < len(deals) and step < nj:
                send_deal()
        x_all = jnp.concatenate(blocks, axis=0)

        def output_chunk(step):
            back = (place - step) % nj
            dest = jnp.where(
                back == 0, 0, jnp.where(back <= nj // 2, 2 * back - 1, 2 * (nj - back))
            )
            part = lax.dynamic_slice(
                attn_all, ((k - dest // per) % nk, 0, (dest % per) * feat), (1, ni * tok, feat)
            )
            return dot_rows(part.reshape(ni * tok, feat), go_all)

        state = {"step": 1, "moving": output_chunk(1).astype(BF16)}

        def send_output():
            moving = lax.ppermute(after(state["moving"], queue[-2]), "ja", ring)
            queue.append(moving)
            state["step"] += 1
            state["total"] = output_chunk(state["step"] % nj) + moving.astype(F32)
            state["moving"] = state["total"].astype(BF16)

        send_output()
        while len(dealt) < len(deals):
            send_deal()

        g_all = jnp.zeros((nj, 2 * tok, 6 * feat), BF16)
        for (step, dy), piece in zip(deals, dealt):
            for hop in range(nk):
                source = per * ((k - hop) % nk) + (j % per - step) % per
                slot = (place - ring_place(source, nj)) % nj
                g_all = lax.dynamic_update_slice(g_all, piece[None], (slot, 0, dy * 3 * feat))
                if hop < nk - 1:
                    piece = lax.ppermute(piece, "ka", core_ring)

        others = []
        for step in range(1, nj + 1):
            other = dot_cols(g_all[step % nj, tok:], w_both).astype(BF16)
            if step > 2:
                other = after(other, others[step - 3])
            others.append(lax.ppermute(other, "ia", swap_x))

        def input_chunk(step):
            return dot_cols(g_all[step % nj, :tok], w_both) + others[step - 1].astype(F32)

        send_output()
        summed = input_chunk(1).astype(BF16)
        for step in range(1, nj):
            summed = lax.ppermute(after(summed, queue[-2]), "ja", ring)
            queue.append(summed)
            summed = (input_chunk(step + 1) + summed.astype(F32)).astype(BF16)
            if state["step"] < nj:
                send_output()
        grad_inputs = summed.reshape(inputs.shape)
        output_weight_grad = state["total"]

        g_flat = g_all.reshape(nj * 2 * tok, 6 * feat)
        weight_grads = []
        for w in range(3):
            other = dot_rows(x_all, g_flat[:, (3 + w) * feat : (4 + w) * feat]).astype(BF16)
            other = lax.ppermute(other, "ia", swap_y)
            weight_grads.append(
                dot_rows(x_all, g_flat[:, w * feat : (w + 1) * feat]) + other.astype(F32)
            )
        return (grad_inputs, *weight_grads, output_weight_grad)

    return local


def solution(mesh):
    return jax.shard_map(
        build(mesh),
        mesh=mesh,
        in_specs=(
            P("ia", "ja", "ka"),
            P(None, "ja", ("ia", "ka")),
            P("ia", "ja", "ka"),
            P(None, "ja", ("ia", "ka")),
            P(None, "ja", ("ia", "ka")),
            P(None, "ja", ("ia", "ka")),
            P("ka", ("ia", "ja")),
            P("ka", ("ia", "ja")),
            P("ka", ("ia", "ja")),
        ),
        out_specs=(
            P("ia", "ja", "ka"),
            P("ka", ("ia", "ja")),
            P("ka", ("ia", "ja")),
            P("ka", ("ia", "ja")),
            P(("ia", "ja"), "ka"),
        ),
        check_vma=False,
    )
```

```python
import jax
import jax.numpy as jnp
from jax import lax
from jax.sharding import PartitionSpec as P

BF16 = jnp.bfloat16
F32 = jnp.float32


def ring_place(j, n):
    return jnp.where(j % 2 == 1, (j + 1) // 2, (n - j // 2) % n)


def ring_pairs(n):
    order = [0] + list(range(1, n, 2)) + list(range(n - 2, 0, -2))
    return [(order[p], order[(p + 1) % n]) for p in range(n)]


def dot_rows(a, b):
    return lax.dot_general(a, b, (((0,), (0,)), ((), ())), preferred_element_type=F32)


def dot_cols(a, b):
    return lax.dot_general(a, b, (((1,), (1,)), ((), ())), preferred_element_type=F32)


def build(mesh):
    ni, nj, nk = mesh.shape["ia"], mesh.shape["ja"], mesh.shape["ka"]
    assert ni == 4 and nj >= 4 and nj % nk == 0
    per = nj // nk
    swap_x = [(i, i ^ 1) for i in range(ni)]
    swap_y = [(i, i ^ 2) for i in range(ni)]
    ring = ring_pairs(nj)
    core_ring = [(k, (k + 1) % nk) for k in range(nk)]

    def deal_pairs(step, dy):
        pairs = []
        for i in range(ni):
            for j in range(nj):
                for k in range(nk):
                    to_j, to_k = per * k + (j + step) % per, j // per
                    pairs.append(
                        ((i * nj + j) * nk + k, ((i ^ (2 * dy)) * nj + to_j) * nk + to_k)
                    )
        return pairs

    def local(
        inputs,
        attn_out,
        grad_out,
        grad_query,
        grad_key,
        grad_value,
        query_weight,
        key_weight,
        value_weight,
    ):
        i, j, k = lax.axis_index("ia"), lax.axis_index("ja"), lax.axis_index("ka")
        tok, width = inputs.shape[1], inputs.shape[2]
        feat = grad_query.shape[2] // per
        place = ring_place(j, nj)
        grads = (grad_query, grad_key, grad_value)

        live = {}

        def gate(**arrived):
            live.update(arrived)
            names = sorted(live)
            live.update(zip(names, lax.optimization_barrier(tuple(live[name] for name in names))))

        def along_x(value):
            return lax.ppermute(value, "ia", swap_x)

        def along_y(value):
            return lax.ppermute(value, "ia", swap_y)

        def along_z(value):
            return lax.ppermute(value, "ja", ring)

        def keep(name, value, *start):
            live[name] = lax.dynamic_update_slice(live[name], value, start)

        deals = [(step, dy) for dy in range(2) for step in range(per)]

        def deal_piece(step, dy):
            chunk = (j + step) % per
            return jnp.concatenate(
                [
                    jnp.concatenate(
                        [
                            lax.dynamic_slice(
                                grad, (i ^ (2 * dy) ^ dx, 0, chunk * feat), (1, tok, feat)
                            ).reshape(tok, feat)
                            for grad in grads
                        ],
                        axis=1,
                    )
                    for dx in range(2)
                ],
                axis=0,
            )

        def deal(index):
            return lax.ppermute(
                live.pop(f"piece{index}"), ("ia", "ja", "ka"), deal_pairs(*deals[index])
            )

        def share(index):
            step, dy = deals[index]
            piece = live.pop(f"dealt{index}")
            for hop in range(nk):
                source = per * ((k - hop) % nk) + (j % per - step) % per
                slot = (place - ring_place(source, nj)) % nj
                keep("g", piece[None], slot, 0, dy * 3 * feat)
                if hop < nk - 1:
                    piece = lax.ppermute(piece, "ka", core_ring)

        def dealt_in(step):
            if step == nj - 1:
                return range(min(step - 1, len(deals)), len(deals))
            return range(step - 1, min(step, len(deals)))

        live["came"] = rows = inputs.reshape(tok, width)
        live["go0"] = grad_out.reshape(tok, width)
        live["wk"], live["wv"] = key_weight, value_weight
        live["g"] = jnp.zeros((nj, 2 * tok, 6 * feat), BF16)
        live["x"] = jnp.zeros((nj * 2 * tok, width), BF16)
        live["w"] = jnp.zeros((width, 6 * feat), BF16)
        live["piece0"] = deal_piece(*deals[0])
        for step in range(1, nj):
            flying = {"came": along_z(live["came"]), "swapped": along_x(live["came"])}
            for index in dealt_in(step):
                flying[f"dealt{index}"] = deal(index)
            if step == 1:
                flying["go1"], flying["go2"] = along_x(live["go0"]), along_y(live["go0"])
                flying["w3"] = along_y(query_weight)
                for index in range(1, len(deals)):
                    live[f"piece{index}"] = deal_piece(*deals[index])
                parts = [
                    jnp.concatenate(
                        [
                            lax.dynamic_index_in_dim(attn_out, i ^ r, 0, keepdims=False)
                            for r in range(ni)
                        ],
                        axis=0,
                    )
                ]
                for _ in range(nk - 1):
                    parts.append(lax.ppermute(parts[-1], "ka", core_ring))
                live["attn"] = jnp.stack(parts)
            elif step == 2:
                flying["go3"] = along_y(live["go1"])
                flying["w4"] = along_y(live["wk"])
                for w, weight in enumerate((query_weight, live.pop("wk"), live["wv"])):
                    keep("w", weight, 0, w * feat)
                keep("w", live.pop("w3"), 0, 3 * feat)
            elif step == 3:
                flying["w5"] = along_y(live.pop("wv"))
                keep("w", live.pop("w4"), 0, 4 * feat)
                live["go"] = jnp.concatenate([live.pop(f"go{r}") for r in range(ni)], axis=0)
            keep("x", live.pop("came"), 2 * (step - 1) * tok, 0)
            if step > 1:
                keep("x", live.pop("swapped"), (2 * step - 3) * tok, 0)
                for index in dealt_in(step - 1):
                    share(index)
            gate(**flying)

        for index in dealt_in(nj - 1):
            share(index)
        keep("w", live.pop("w5"), 0, 5 * feat)

        def output_chunk(step):
            back = (place - step) % nj
            dest = jnp.where(
                back == 0, 0, jnp.where(back <= nj // 2, 2 * back - 1, 2 * (nj - back))
            )
            part = lax.dynamic_slice(
                live["attn"],
                ((k - dest // per) % nk, 0, (dest % per) * feat),
                (1, ni * tok, feat),
            )
            return dot_rows(part.reshape(ni * tok, feat), live["go"])

        def other_chunk(step):
            return dot_cols(live["g"][step % nj, tok:], live["w"]).astype(BF16)

        def own_chunk(step):
            return dot_cols(live["g"][step % nj, :tok], live["w"])

        def weight_term(w, count):
            part = live["g"][:, :, w * feat : (w + count) * feat]
            return dot_rows(live["x"], part.reshape(nj * 2 * tok, count * feat))

        flying = {"out": along_z(output_chunk(1).astype(BF16)), "other": along_x(other_chunk(1))}
        keep("x", live.pop("swapped"), (2 * nj - 3) * tok, 0)
        keep("x", live["came"], (2 * nj - 2) * tok, 0)
        live["own"] = own_chunk(1)
        live["part"] = output_chunk(2)
        live["send"] = other_chunk(2)
        gate(**flying)

        for step in range(1, nj):
            own = live.pop("own") + live.pop("other").astype(F32)
            if step > 1:
                own = own + live.pop("sum").astype(F32)
            total = live.pop("part") + live.pop("out").astype(F32)
            flying = {"sum": along_z(own.astype(BF16)), "other": along_x(live.pop("send"))}
            if step < nj - 1:
                flying["out"] = along_z(total.astype(BF16))
                live["part"] = output_chunk((step + 2) % nj)
                live["send"] = other_chunk(step + 2)
            else:
                output_weight_grad = total
            live["own"] = own_chunk(step + 1)
            if step == 1:
                flying["swapped"] = along_x(live.pop("came"))
            elif step == 2:
                keep("x", live.pop("swapped"), (2 * nj - 1) * tok, 0)
                flying["query"] = along_y(weight_term(3, 1).astype(BF16))
                flying["key"] = along_y(weight_term(4, 1).astype(BF16))
            elif step == 3:
                flying["value"] = along_y(weight_term(5, 1).astype(BF16))
                query_weight_grad = weight_term(0, 1) + live.pop("query").astype(F32)
                key_weight_grad = weight_term(1, 1) + live.pop("key").astype(F32)
            gate(**flying)
        grad_inputs = live["own"] + live["other"].astype(F32) + live["sum"].astype(F32)
        grad_inputs = grad_inputs.astype(BF16).reshape(inputs.shape)
        value_weight_grad = weight_term(2, 1) + live["value"].astype(F32)
        weight_grads = (query_weight_grad, key_weight_grad, value_weight_grad)
        return (grad_inputs, *weight_grads, output_weight_grad)

    return local


def solution(mesh):
    return jax.shard_map(
        build(mesh),
        mesh=mesh,
        in_specs=(
            P("ia", "ja", "ka"),
            P(None, "ja", ("ia", "ka")),
            P("ia", "ja", "ka"),
            P(None, "ja", ("ia", "ka")),
            P(None, "ja", ("ia", "ka")),
            P(None, "ja", ("ia", "ka")),
            P("ka", ("ia", "ja")),
            P("ka", ("ia", "ja")),
            P("ka", ("ia", "ja")),
        ),
        out_specs=(
            P("ia", "ja", "ka"),
            P("ka", ("ia", "ja")),
            P("ka", ("ia", "ja")),
            P("ka", ("ia", "ja")),
            P(("ia", "ja"), "ka"),
        ),
        check_vma=False,
    )
```

```python
import jax
import jax.numpy as jnp
from jax import lax
from jax.sharding import PartitionSpec as P

BF16 = jnp.bfloat16
F32 = jnp.float32


def ring_place(j, n):
    return jnp.where(j % 2 == 1, (j + 1) // 2, (n - j // 2) % n)


def ring_device(place, n):
    return jnp.where(
        place == 0, 0, jnp.where(place <= n // 2, 2 * place - 1, 2 * (n - place))
    )


def ring_pairs(n):
    order = [0] + list(range(1, n, 2)) + list(range(n - 2, 0, -2))
    return [(order[p], order[(p + 1) % n]) for p in range(n)]


def dot_rows(a, b):
    return lax.dot_general(a, b, (((0,), (0,)), ((), ())), preferred_element_type=F32)


def dot_cols(a, b):
    return lax.dot_general(a, b, (((1,), (1,)), ((), ())), preferred_element_type=F32)


def build(mesh):
    ni, nj, nk = mesh.shape["ia"], mesh.shape["ja"], mesh.shape["ka"]
    assert ni == 4 and nj >= 4 and nj % nk == 0
    per = nj // nk
    swap_x = [(i, i ^ 1) for i in range(ni)]
    swap_y = [(i, i ^ 2) for i in range(ni)]
    right = [(j, j + 1) for j in range(nj - 1)]
    left = [(j + 1, j) for j in range(nj - 1)]
    ring = ring_pairs(nj)
    core_ring = [(k, (k + 1) % nk) for k in range(nk)]

    def deal_pairs(step, dy):
        pairs = []
        for i in range(ni):
            for j in range(nj):
                for k in range(nk):
                    to_j, to_k = per * k + (j + step) % per, j // per
                    pairs.append(
                        ((i * nj + j) * nk + k, ((i ^ (2 * dy)) * nj + to_j) * nk + to_k)
                    )
        return pairs

    def local(
        inputs,
        attn_out,
        grad_out,
        grad_query,
        grad_key,
        grad_value,
        query_weight,
        key_weight,
        value_weight,
    ):
        i, j, k = lax.axis_index("ia"), lax.axis_index("ja"), lax.axis_index("ka")
        tok, width = inputs.shape[1], inputs.shape[2]
        feat = grad_query.shape[2] // per
        grads = (grad_query, grad_key, grad_value)

        live = {"token": value_weight}

        def gate(names, *values):
            names = [name for name in names if name in live] + ["token"]
            out = lax.optimization_barrier(tuple(live[name] for name in names) + values)
            live.update(zip(names, out))
            return out[len(names) :]

        def along_x(value):
            return lax.ppermute(value, "ia", swap_x)

        def along_y(value):
            return lax.ppermute(value, "ia", swap_y)

        def along_z(name, to_right, to_left):
            live[name + "_r"] = lax.ppermute(to_right, "ja", right)
            live[name + "_l"] = lax.ppermute(to_left, "ja", left)

        def keep(name, value, *start):
            live[name] = lax.dynamic_update_slice(live[name], value, start)

        def slot_of(source):
            return jnp.where(
                source == j, 0, jnp.where(source > j, source - j, nj - 1 - source)
            )

        deals = [(step, dy) for dy in range(2) for step in range(per)]

        def deal_piece(step, dy):
            chunk = (j + step) % per
            return jnp.concatenate(
                [
                    jnp.concatenate(
                        [
                            lax.dynamic_slice(
                                grad, (i ^ (2 * dy) ^ dx, 0, chunk * feat), (1, tok, feat)
                            ).reshape(tok, feat)
                            for grad in grads
                        ],
                        axis=1,
                    )
                    for dx in range(2)
                ],
                axis=0,
            )

        def deal(index, piece):
            live[f"dealt{index}"] = lax.ppermute(piece, ("ia", "ja", "ka"), deal_pairs(*deals[index]))

        def share(indices):
            if len(indices) == 0:
                return
            pieces = [live[f"dealt{index}"].reshape(2, 1, tok, 3 * feat) for index in indices]
            pieces = jnp.concatenate(pieces, axis=1)
            for hop in range(nk):
                for place_in, index in enumerate(indices):
                    step, dy = deals[index]
                    source = per * ((k - hop) % nk) + (j % per - step) % per
                    piece = pieces[:, place_in : place_in + 1]
                    keep("g", piece, 0, slot_of(source), 0, dy * 3 * feat)
                if hop < nk - 1:
                    pieces = lax.ppermute(pieces, "ka", core_ring)

        rows = inputs.reshape(tok, width)
        go_own = grad_out.reshape(tok, width)
        high = max(tok, feat)

        def fill(block):
            return jnp.pad(block, ((0, high - block.shape[0]), (0, 0)))

        along_z("line1", fill(rows), fill(rows))
        live["go2"] = along_y(go_own)
        live["go1"] = along_x(go_own)
        deal(0, deal_piece(*deals[0]))
        pieces = [deal_piece(*deals[index]) for index in range(1, len(deals))]

        def next_deal(index):
            if 0 < index < len(deals):
                (piece,) = gate([f"dealt{index - 1}"], pieces[index - 1])
                deal(index, piece)

        (go_next, weight) = gate(["go1", "go2"], live["go2"], query_weight)
        live["go2"] = go_next
        live["go3"] = along_x(go_next)
        live["wq"] = along_y(weight)
        next_deal(1)

        def block_of(step):
            block = live[f"line{step}_l"]
            for near in range(1, step + 1):
                block = jnp.where(j == nj - 1 - step + near, live[f"line{near}_r"], block)
            return block[:tok]

        part = jnp.concatenate(
            [lax.dynamic_index_in_dim(attn_out, i ^ r, 0, keepdims=False) for r in range(ni)], axis=0
        )
        parts = [part]
        for _ in range(nk - 1):
            parts.append(lax.ppermute(parts[-1], "ka", core_ring))
        attn = jnp.concatenate(parts, axis=1)

        gate(["line1_r", "line1_l"])
        block, weight = gate(["go3", "wq"], block_of(1), key_weight)
        live["block1"] = block
        live["swap1"] = along_x(block)
        live["wk"] = along_y(weight)
        go = jnp.concatenate((go_own, live["go1"], live["go2"], live["go3"]), axis=0)
        output_terms = dot_rows(attn, go)

        def output_chunk(dest):
            start = (((k - dest // per) % nk) * per + dest % per) * feat
            return lax.dynamic_slice(output_terms, (start, 0), (feat, width))

        def next_line(step):
            part_r = output_chunk(jnp.minimum(nj - step + j, nj - 1))
            part_l = output_chunk(jnp.maximum(step + j - nj, 0))
            part_r = fill(jnp.where(j < step, part_r, 0.0))
            part_l = fill(jnp.where(j >= nj - step, part_l, 0.0))
            to_right = (live[f"line{step}_r"].astype(F32) + part_r).astype(BF16)
            to_left = (live[f"line{step}_l"].astype(F32) + part_l).astype(BF16)
            along_z(f"line{step + 1}", to_right, to_left)

        next_line(1)
        next_deal(2)
        mine, weight = gate(["swap1", "wk"], rows, value_weight)
        live["swap0"] = along_x(mine)
        live["wv"] = along_y(weight)
        for index in range(3, len(deals)):
            next_deal(index)
        live["g"] = jnp.zeros((2, nj, tok, 6 * feat), BF16)
        for step in range(2, nj):
            gate([f"line{step}_r", f"line{step}_l"])
            next_line(step)
            names = ["swap0", "wv"] if step == 2 else [f"swap{step - 1}"]
            (block,) = gate(names, block_of(step))
            live[f"block{step}"] = block
            live[f"swap{step}"] = along_x(block)
            if step == 2:
                share(range(0, min(2, len(deals))))
                gate([f"dealt{len(deals) - 1}"])
                share(range(2, len(deals)))
        w = jnp.concatenate(
            (query_weight, key_weight, live["token"], live["wq"], live["wk"], live["wv"]), axis=1
        )

        place = ring_place(j, nj)
        halves = [slice(0, width // 2), slice(width // 2, width)]

        def chunk(bank, step, half):
            dest = ring_device((place - step) % nj, nj)
            part = lax.dynamic_index_in_dim(live["g"][bank], slot_of(dest), 0, keepdims=False)
            return dot_cols(part, w[halves[half]])

        x_all = jnp.concatenate(
            [rows]
            + [live[f"block{step}"] for step in range(1, nj)]
            + [live[f"swap{step}"] for step in range(nj)],
            axis=0,
        )

        def weight_term(w, count):
            part = live["g"].reshape(2 * nj * tok, 6 * feat)
            return dot_rows(x_all, part[:, w * feat : (w + count) * feat])

        live["pair"] = along_y(weight_term(3, 2).astype(BF16))
        value = weight_term(5, 1).astype(BF16)

        others = [[], []]
        sums = [None, None]
        for step in range(1, nj + 1):
            for half in range(2):
                if step == 1 and half == 1:
                    name = f"swap{nj - 1}"
                    live["g"], live[name] = lax.optimization_barrier((live["g"], live[name]))
                elif step > 2:
                    live["g"], others[half][step - 3] = lax.optimization_barrier(
                        (live["g"], others[half][step - 3])
                    )
                other = chunk(1, step, half).astype(BF16)
                if step == nj and half == 0:
                    live["pair"], value, other = lax.optimization_barrier(
                        (live["pair"], value, other)
                    )
                    value = along_y(value)
                if step > 1:
                    others[half][-1], other = lax.optimization_barrier((others[half][-1], other))
                others[half].append(along_x(other))
            for half in range(2):
                if step > 1:
                    term = chunk(0, step - 1, half) + others[half][step - 2].astype(F32)
                    term = lax.optimization_barrier(term)
                    if step > 2:
                        term = term + sums[half].astype(F32)
                    sums[half] = lax.ppermute(term.astype(BF16), "ja", ring)
        final = []
        for half in range(2):
            term = chunk(0, nj, half) + others[half][nj - 1].astype(F32)
            term = lax.optimization_barrier(term)
            final.append((term + sums[half].astype(F32)).astype(BF16))
        grad_inputs = jnp.concatenate(final, axis=1).reshape(inputs.shape)
        from_ends = live[f"line{nj}_r"].astype(F32) + live[f"line{nj}_l"].astype(F32)
        output_weight_grad = output_chunk(j) + from_ends[:feat]

        weight_grads = (
            weight_term(0, 1) + live["pair"][:, :feat].astype(F32),
            weight_term(1, 1) + live["pair"][:, feat:].astype(F32),
            weight_term(2, 1) + value.astype(F32),
        )
        return (grad_inputs, *weight_grads, output_weight_grad)

    return local


def solution(mesh):
    return jax.shard_map(
        build(mesh),
        mesh=mesh,
        in_specs=(
            P("ia", "ja", "ka"),
            P(None, "ja", ("ia", "ka")),
            P("ia", "ja", "ka"),
            P(None, "ja", ("ia", "ka")),
            P(None, "ja", ("ia", "ka")),
            P(None, "ja", ("ia", "ka")),
            P("ka", ("ia", "ja")),
            P("ka", ("ia", "ja")),
            P("ka", ("ia", "ja")),
        ),
        out_specs=(
            P("ia", "ja", "ka"),
            P("ka", ("ia", "ja")),
            P("ka", ("ia", "ja")),
            P("ka", ("ia", "ja")),
            P(("ia", "ja"), "ka"),
        ),
        check_vma=False,
    )
```

```python
import jax
import jax.numpy as jnp
from jax import lax
from jax.sharding import PartitionSpec as P

BF16 = jnp.bfloat16
F32 = jnp.float32


def ring_place(j, n):
    return jnp.where(j % 2 == 1, (j + 1) // 2, (n - j // 2) % n)


def ring_device(place, n):
    return jnp.where(
        place == 0, 0, jnp.where(place <= n // 2, 2 * place - 1, 2 * (n - place))
    )


def ring_pairs(n):
    order = [0] + list(range(1, n, 2)) + list(range(n - 2, 0, -2))
    return [(order[p], order[(p + 1) % n]) for p in range(n)]


def dot_rows(a, b):
    return lax.dot_general(a, b, (((0,), (0,)), ((), ())), preferred_element_type=F32)


def dot_cols(a, b):
    return lax.dot_general(a, b, (((1,), (1,)), ((), ())), preferred_element_type=F32)


def build(mesh):
    ni, nj, nk = mesh.shape["ia"], mesh.shape["ja"], mesh.shape["ka"]
    assert ni == 4 and nj >= 4 and nj % nk == 0
    per = nj // nk
    swap_x = [(i, i ^ 1) for i in range(ni)]
    swap_y = [(i, i ^ 2) for i in range(ni)]
    right = [(j, j + 1) for j in range(nj - 1)]
    left = [(j + 1, j) for j in range(nj - 1)]
    ring = ring_pairs(nj)
    core_ring = [(k, (k + 1) % nk) for k in range(nk)]

    def deal_pairs(step, dy):
        pairs = []
        for i in range(ni):
            for j in range(nj):
                for k in range(nk):
                    to_j, to_k = per * k + (j + step) % per, j // per
                    pairs.append(
                        ((i * nj + j) * nk + k, ((i ^ (2 * dy)) * nj + to_j) * nk + to_k)
                    )
        return pairs

    def local(
        inputs,
        attn_out,
        grad_out,
        grad_query,
        grad_key,
        grad_value,
        query_weight,
        key_weight,
        value_weight,
    ):
        i, j, k = lax.axis_index("ia"), lax.axis_index("ja"), lax.axis_index("ka")
        tok, width = inputs.shape[1], inputs.shape[2]
        feat = grad_query.shape[2] // per
        grads = (grad_query, grad_key, grad_value)

        live, before = {}, {}

        def send(stream, after=(), **values):
            earlier = before.get(stream, []) + [name for name in after if name in live]
            names = list(values)
            out = lax.optimization_barrier(
                tuple(values[name] for name in names) + tuple(live[name] for name in earlier)
            )
            live.update(zip(earlier, out[len(names) :]))
            before[stream] = names
            return out[: len(names)]

        def along_x(name, value, after=()):
            (value,) = send("x", after, **{name: value})
            live[name] = lax.ppermute(value, "ia", swap_x)

        def along_y(name, value, after=()):
            (value,) = send("y", after, **{name: value})
            live[name] = lax.ppermute(value, "ia", swap_y)

        def along_z(name, to_right, to_left, after=()):
            to_right, to_left = send("z", after, **{name + "_r": to_right, name + "_l": to_left})
            live[name + "_r"] = lax.ppermute(to_right, "ja", right)
            live[name + "_l"] = lax.ppermute(to_left, "ja", left)

        def keep(name, value, *start):
            live[name] = lax.dynamic_update_slice(live[name], value, start)

        def slot_of(source):
            return jnp.where(
                source == j, 0, jnp.where(source > j, source - j, nj - 1 - source)
            )

        deals = [(step, dy) for dy in range(2) for step in range(per)]

        def deal_piece(step, dy):
            chunk = (j + step) % per
            return jnp.concatenate(
                [
                    jnp.concatenate(
                        [
                            lax.dynamic_slice(
                                grad, (i ^ (2 * dy) ^ dx, 0, chunk * feat), (1, tok, feat)
                            ).reshape(tok, feat)
                            for grad in grads
                        ],
                        axis=1,
                    )
                    for dx in range(2)
                ],
                axis=0,
            )

        def deal(index):
            name = f"dealt{index}"
            (piece,) = send("deal", **{name: deal_piece(*deals[index])})
            live[name] = lax.ppermute(piece, ("ia", "ja", "ka"), deal_pairs(*deals[index]))

        def share(indices):
            if len(indices) == 0:
                return
            pieces = [live[f"dealt{index}"].reshape(2, 1, tok, 3 * feat) for index in indices]
            pieces = jnp.concatenate(pieces, axis=1)
            for hop in range(nk):
                for place_in, index in enumerate(indices):
                    step, dy = deals[index]
                    source = per * ((k - hop) % nk) + (j % per - step) % per
                    piece = pieces[:, place_in : place_in + 1]
                    keep("g", piece, 0, slot_of(source), 0, dy * 3 * feat)
                if hop < nk - 1:
                    pieces = lax.ppermute(pieces, "ka", core_ring)

        rows = inputs.reshape(tok, width)
        go_own = grad_out.reshape(tok, width)
        high = max(tok, feat)

        def fill(block):
            return jnp.pad(block, ((0, high - block.shape[0]), (0, 0)))

        along_z("line1", fill(rows), fill(rows))
        along_y("go2", go_own)
        along_x("go1", go_own)
        deal(0)
        along_y("wq", query_weight)
        along_x("go3", live["go2"])
        along_x("swap0", rows, ("dealt0", "line1_r", "line1_l"))
        deal(1)
        along_y("wk", key_weight)
        along_y("wv", value_weight)

        go = jnp.concatenate((go_own, live["go1"], live["go2"], live["go3"]), axis=0)
        parts = [
            jnp.concatenate(
                [lax.dynamic_index_in_dim(attn_out, i ^ r, 0, keepdims=False) for r in range(ni)],
                axis=0,
            )
        ]
        for _ in range(nk - 1):
            parts.append(lax.ppermute(parts[-1], "ka", core_ring))
        output_terms = dot_rows(jnp.concatenate(parts, axis=1), go)

        def output_chunk(dest):
            start = (((k - dest // per) % nk) * per + dest % per) * feat
            return lax.dynamic_slice(output_terms, (start, 0), (feat, width))

        live["g"] = jnp.zeros((2, nj, tok, 6 * feat), BF16)
        live["x"] = jnp.zeros((2 * nj * tok, width), BF16)
        keep("x", rows, 0, 0)
        come = {"r": [], "l": []}
        for step in range(1, nj + 1):
            for side in "rl":
                come[side].append(f"line{step}_{side}")
            if step < nj:
                part_r = output_chunk(jnp.minimum(nj - step + j, nj - 1))
                part_l = output_chunk(jnp.maximum(step + j - nj, 0))
                part_r = fill(jnp.where(j < step, part_r, 0.0))
                part_l = fill(jnp.where(j >= nj - step, part_l, 0.0))
                to_right = (live[f"line{step}_r"].astype(F32) + part_r).astype(BF16)
                to_left = (live[f"line{step}_l"].astype(F32) + part_l).astype(BF16)
                along_z(f"line{step + 1}", to_right, to_left)
                block = live[f"line{step}_l"]
                for near in range(1, step + 1):
                    block = jnp.where(j == nj - 1 - step + near, live[f"line{near}_r"], block)
                block = block[:tok]
                after = {1: ("wq",), 2: ("dealt1", "wk"), 3: ("dealt2", "wv")}
                along_x(f"swap{step}", block, after.get(step, ()))
                keep("x", block, step * tok, 0)
                keep("x", live[f"swap{step - 1}"], (nj + step - 1) * tok, 0)
            if step < 3:
                for index in range(step + 1, len(deals) if step == 2 else min(step + 2, len(deals))):
                    deal(index)
            if step == 2:
                share(range(0, min(2, len(deals))))
        share(range(2, len(deals)))
        w = jnp.concatenate(
            (query_weight, key_weight, value_weight, live["wq"], live["wk"], live["wv"]), axis=1
        )

        place = ring_place(j, nj)

        def chunk(bank, step):
            dest = ring_device((place - step) % nj, nj)
            part = lax.dynamic_index_in_dim(live["g"][bank], slot_of(dest), 0, keepdims=False)
            return dot_cols(part, w)

        def weight_term(w, count):
            part = live["g"].reshape(2 * nj * tok, 6 * feat)
            return dot_rows(live["x"], part[:, w * feat : (w + count) * feat])

        along_x("other1", chunk(1, 1).astype(BF16))
        keep("x", live[f"swap{nj - 1}"], (2 * nj - 1) * tok, 0)
        along_y("pair", weight_term(3, 2).astype(BF16))
        for step in range(2, nj + 1):
            along_x(
                f"other{step}", chunk(1, step).astype(BF16), ("pair",) if step == nj else ()
            )
            term = chunk(0, step - 1) + live[f"other{step - 1}"].astype(F32)
            if step > 2:
                term = lax.optimization_barrier(term) + live[f"sum{step - 2}"].astype(F32)
            (term,) = send("sum", **{f"sum{step - 1}": term.astype(BF16)})
            live[f"sum{step - 1}"] = lax.ppermute(term, "ja", ring)
        along_y("value", weight_term(5, 1).astype(BF16))
        grad_inputs = chunk(0, nj) + live[f"other{nj}"].astype(F32)
        grad_inputs = lax.optimization_barrier(grad_inputs) + live[f"sum{nj - 1}"].astype(F32)
        grad_inputs = grad_inputs.astype(BF16).reshape(inputs.shape)
        from_ends = live[f"line{nj}_r"].astype(F32) + live[f"line{nj}_l"].astype(F32)
        output_weight_grad = output_chunk(j) + from_ends[:feat]
        weight_grads = (
            weight_term(0, 1) + live["pair"][:, :feat].astype(F32),
            weight_term(1, 1) + live["pair"][:, feat:].astype(F32),
            weight_term(2, 1) + live["value"].astype(F32),
        )
        return (grad_inputs, *weight_grads, output_weight_grad)

    return local


def solution(mesh):
    return jax.shard_map(
        build(mesh),
        mesh=mesh,
        in_specs=(
            P("ia", "ja", "ka"),
            P(None, "ja", ("ia", "ka")),
            P("ia", "ja", "ka"),
            P(None, "ja", ("ia", "ka")),
            P(None, "ja", ("ia", "ka")),
            P(None, "ja", ("ia", "ka")),
            P("ka", ("ia", "ja")),
            P("ka", ("ia", "ja")),
            P("ka", ("ia", "ja")),
        ),
        out_specs=(
            P("ia", "ja", "ka"),
            P("ka", ("ia", "ja")),
            P("ka", ("ia", "ja")),
            P("ka", ("ia", "ja")),
            P(("ia", "ja"), "ka"),
        ),
        check_vma=False,
    )
```

```python
import jax
import jax.numpy as jnp
from jax import lax
from jax.sharding import PartitionSpec as P

BF16 = jnp.bfloat16
F32 = jnp.float32


def ring_place(j, n):
    return jnp.where(j % 2 == 1, (j + 1) // 2, (n - j // 2) % n)


def ring_device(place, n):
    return jnp.where(
        place == 0, 0, jnp.where(place <= n // 2, 2 * place - 1, 2 * (n - place))
    )


def ring_pairs(n):
    order = [0] + list(range(1, n, 2)) + list(range(n - 2, 0, -2))
    return [(order[p], order[(p + 1) % n]) for p in range(n)]


def dot_rows(a, b):
    return lax.dot_general(a, b, (((0,), (0,)), ((), ())), preferred_element_type=F32)


def dot_cols(a, b):
    return lax.dot_general(a, b, (((1,), (1,)), ((), ())), preferred_element_type=F32)


def build(mesh):
    ni, nj, nk = mesh.shape["ia"], mesh.shape["ja"], mesh.shape["ka"]
    assert ni == 4 and nj >= 4 and nj % nk == 0
    per = nj // nk
    swap_x = [(i, i ^ 1) for i in range(ni)]
    swap_y = [(i, i ^ 2) for i in range(ni)]
    right = [(j, j + 1) for j in range(nj - 1)]
    left = [(j + 1, j) for j in range(nj - 1)]
    ring = ring_pairs(nj)
    core_ring = [(k, (k + 1) % nk) for k in range(nk)]

    def deal_pairs(step, dy):
        pairs = []
        for i in range(ni):
            for j in range(nj):
                for k in range(nk):
                    to_j, to_k = per * k + (j + step) % per, j // per
                    pairs.append(
                        ((i * nj + j) * nk + k, ((i ^ (2 * dy)) * nj + to_j) * nk + to_k)
                    )
        return pairs

    def local(
        inputs,
        attn_out,
        grad_out,
        grad_query,
        grad_key,
        grad_value,
        query_weight,
        key_weight,
        value_weight,
    ):
        i, j, k = lax.axis_index("ia"), lax.axis_index("ja"), lax.axis_index("ka")
        tok, width = inputs.shape[1], inputs.shape[2]
        feat = grad_query.shape[2] // per
        grads = (grad_query, grad_key, grad_value)

        live, before = {}, {}

        def send(stream, after=(), **values):
            earlier = before.get(stream, []) + [name for name in after if name in live]
            names = list(values)
            out = lax.optimization_barrier(
                tuple(values[name] for name in names) + tuple(live[name] for name in earlier)
            )
            live.update(zip(earlier, out[len(names) :]))
            before[stream] = names
            return out[: len(names)]

        def along_x(name, value, after=()):
            (value,) = send("x", after, **{name: value})
            live[name] = lax.ppermute(value, "ia", swap_x)

        def along_y(name, value, after=()):
            (value,) = send("y", after, **{name: value})
            live[name] = lax.ppermute(value, "ia", swap_y)

        def along_z(name, to_right, to_left, after=()):
            to_right, to_left = send("z", after, **{name + "_r": to_right, name + "_l": to_left})
            live[name + "_r"] = lax.ppermute(to_right, "ja", right)
            live[name + "_l"] = lax.ppermute(to_left, "ja", left)

        def keep(name, value, *start):
            live[name] = lax.dynamic_update_slice(live[name], value, start)

        def slot_of(source):
            return jnp.where(
                source == j, 0, jnp.where(source > j, source - j, nj - 1 - source)
            )

        deals = [(step, dy) for dy in range(2) for step in range(per)]

        def deal_piece(step, dy):
            chunk = (j + step) % per
            return jnp.concatenate(
                [
                    jnp.concatenate(
                        [
                            lax.dynamic_slice(
                                grad, (i ^ (2 * dy) ^ dx, 0, chunk * feat), (1, tok, feat)
                            ).reshape(tok, feat)
                            for grad in grads
                        ],
                        axis=1,
                    )
                    for dx in range(2)
                ],
                axis=0,
            )

        def deal(index):
            name = f"dealt{index}"
            (piece,) = send("deal", **{name: deal_piece(*deals[index])})
            live[name] = lax.ppermute(piece, ("ia", "ja", "ka"), deal_pairs(*deals[index]))

        def share(indices):
            if len(indices) == 0:
                return
            pieces = [live[f"dealt{index}"].reshape(2, 1, tok, 3 * feat) for index in indices]
            pieces = jnp.concatenate(pieces, axis=1)
            for hop in range(nk):
                for place_in, index in enumerate(indices):
                    step, dy = deals[index]
                    source = per * ((k - hop) % nk) + (j % per - step) % per
                    piece = pieces[:, place_in : place_in + 1]
                    keep("g", piece, 0, slot_of(source), 0, dy * 3 * feat)
                if hop < nk - 1:
                    pieces = lax.ppermute(pieces, "ka", core_ring)

        rows = inputs.reshape(tok, width)
        go_own = grad_out.reshape(tok, width)
        high = max(tok, feat)

        def fill(block):
            return jnp.pad(block, ((0, high - block.shape[0]), (0, 0)))

        along_z("line1", fill(rows), fill(rows))
        along_y("go2", go_own)
        along_x("go1", go_own)
        deal(0)
        along_y("wq", query_weight)
        along_x("go3", live["go2"])
        (mine,) = send("own", ("dealt0",), swap0=rows)
        live["swap0"] = lax.ppermute(mine, "ia", swap_x)
        deal(1)
        along_y("wk", key_weight)
        along_y("wv", value_weight)

        part = jnp.concatenate(
            [lax.dynamic_index_in_dim(attn_out, i ^ r, 0, keepdims=False) for r in range(ni)], axis=0
        )
        parts = list(send("attn", ("go1",), attn=part))
        go = jnp.concatenate((go_own, live["go1"], live["go2"], live["go3"]), axis=0)
        for _ in range(nk - 1):
            parts.append(lax.ppermute(parts[-1], "ka", core_ring))
        output_terms = dot_rows(jnp.concatenate(parts, axis=1), go)

        def output_chunk(dest):
            start = (((k - dest // per) % nk) * per + dest % per) * feat
            return lax.dynamic_slice(output_terms, (start, 0), (feat, width))

        live["g"] = jnp.zeros((2, nj, tok, 6 * feat), BF16)
        live["x"] = jnp.zeros((2 * nj * tok, width), BF16)
        keep("x", rows, 0, 0)
        come = {"r": [], "l": []}
        for step in range(1, nj + 1):
            for side in "rl":
                come[side].append(f"line{step}_{side}")
            if step < nj:
                part_r = output_chunk(jnp.minimum(nj - step + j, nj - 1))
                part_l = output_chunk(jnp.maximum(step + j - nj, 0))
                part_r = fill(jnp.where(j < step, part_r, 0.0))
                part_l = fill(jnp.where(j >= nj - step, part_l, 0.0))
                to_right = (live[f"line{step}_r"].astype(F32) + part_r).astype(BF16)
                to_left = (live[f"line{step}_l"].astype(F32) + part_l).astype(BF16)
                after = {1: ("dealt1",), 3: ("dealt3",)}
                along_z(f"line{step + 1}", to_right, to_left, after.get(step, ()))
                block = live[f"line{step}_l"]
                for near in range(1, step + 1):
                    block = jnp.where(j == nj - 1 - step + near, live[f"line{near}_r"], block)
                block = block[:tok]
                after = {1: ("wq",), 2: ("swap0", "wk"), 3: ("dealt2", "wv")}
                along_x(f"swap{step}", block, after.get(step, ()))
                keep("x", block, step * tok, 0)
                if step > 1:
                    keep("x", live[f"swap{step - 1}"], (nj + step - 1) * tok, 0)
            if step < 3:
                for index in range(step + 1, len(deals) if step == 2 else min(step + 2, len(deals))):
                    deal(index)
            if step == 2:
                share(range(0, min(2, len(deals))))
        share(range(2, len(deals)))
        keep("x", live["swap0"], nj * tok, 0)
        w = jnp.concatenate(
            (query_weight, key_weight, value_weight, live["wq"], live["wk"], live["wv"]), axis=1
        )

        place = ring_place(j, nj)

        def chunk(bank, step):
            dest = ring_device((place - step) % nj, nj)
            part = lax.dynamic_index_in_dim(live["g"][bank], slot_of(dest), 0, keepdims=False)
            return dot_cols(part, w)

        def weight_term(w, count, first=0, end=2 * nj * tok):
            part = live["g"].reshape(2 * nj * tok, 6 * feat)
            return dot_rows(live["x"][first:end], part[first:end, w * feat : (w + count) * feat])

        last = (2 * nj - 1) * tok
        pair = lax.optimization_barrier(weight_term(3, 2, 0, last))
        along_x("other1", chunk(1, 1).astype(BF16))
        keep("x", live[f"swap{nj - 1}"], last, 0)
        along_y("pair", (pair + weight_term(3, 2, last)).astype(BF16))
        for step in range(2, nj + 1):
            along_x(
                f"other{step}", chunk(1, step).astype(BF16), ("pair",) if step == nj else ()
            )
            term = chunk(0, step - 1) + live[f"other{step - 1}"].astype(F32)
            if step > 2:
                term = lax.optimization_barrier(term) + live[f"sum{step - 2}"].astype(F32)
            (term,) = send("sum", **{f"sum{step - 1}": term.astype(BF16)})
            live[f"sum{step - 1}"] = lax.ppermute(term, "ja", ring)
        along_y("value", weight_term(5, 1).astype(BF16))
        grad_inputs = chunk(0, nj) + live[f"other{nj}"].astype(F32)
        grad_inputs = lax.optimization_barrier(grad_inputs) + live[f"sum{nj - 1}"].astype(F32)
        grad_inputs = grad_inputs.astype(BF16).reshape(inputs.shape)
        from_ends = live[f"line{nj}_r"].astype(F32) + live[f"line{nj}_l"].astype(F32)
        output_weight_grad = output_chunk(j) + from_ends[:feat]
        weight_grads = (
            weight_term(0, 1) + live["pair"][:, :feat].astype(F32),
            weight_term(1, 1) + live["pair"][:, feat:].astype(F32),
            weight_term(2, 1) + live["value"].astype(F32),
        )
        return (grad_inputs, *weight_grads, output_weight_grad)

    return local


def solution(mesh):
    return jax.shard_map(
        build(mesh),
        mesh=mesh,
        in_specs=(
            P("ia", "ja", "ka"),
            P(None, "ja", ("ia", "ka")),
            P("ia", "ja", "ka"),
            P(None, "ja", ("ia", "ka")),
            P(None, "ja", ("ia", "ka")),
            P(None, "ja", ("ia", "ka")),
            P("ka", ("ia", "ja")),
            P("ka", ("ia", "ja")),
            P("ka", ("ia", "ja")),
        ),
        out_specs=(
            P("ia", "ja", "ka"),
            P("ka", ("ia", "ja")),
            P("ka", ("ia", "ja")),
            P("ka", ("ia", "ja")),
            P(("ia", "ja"), "ka"),
        ),
        check_vma=False,
    )
```

```python
import jax
import jax.numpy as jnp
from jax import lax
from jax.sharding import PartitionSpec as P

BF16 = jnp.bfloat16
F32 = jnp.float32


def ring_place(j, n):
    return jnp.where(j % 2 == 1, (j + 1) // 2, (n - j // 2) % n)


def ring_device(place, n):
    return jnp.where(
        place == 0, 0, jnp.where(place <= n // 2, 2 * place - 1, 2 * (n - place))
    )


def ring_pairs(n):
    order = [0] + list(range(1, n, 2)) + list(range(n - 2, 0, -2))
    return [(order[p], order[(p + 1) % n]) for p in range(n)]


def dot_rows(a, b):
    return lax.dot_general(a, b, (((0,), (0,)), ((), ())), preferred_element_type=F32)


def dot_cols(a, b):
    return lax.dot_general(a, b, (((1,), (1,)), ((), ())), preferred_element_type=F32)


def build(mesh):
    ni, nj, nk = mesh.shape["ia"], mesh.shape["ja"], mesh.shape["ka"]
    assert ni == 4 and nj >= 4 and nj % nk == 0
    per = nj // nk
    swap_x = [(i, i ^ 1) for i in range(ni)]
    swap_y = [(i, i ^ 2) for i in range(ni)]
    right = [(j, j + 1) for j in range(nj - 1)]
    left = [(j + 1, j) for j in range(nj - 1)]
    ring = ring_pairs(nj)
    core_ring = [(k, (k + 1) % nk) for k in range(nk)]

    def deal_pairs(step, dy):
        pairs = []
        for i in range(ni):
            for j in range(nj):
                for k in range(nk):
                    to_j, to_k = per * k + (j + step) % per, j // per
                    pairs.append(
                        ((i * nj + j) * nk + k, ((i ^ (2 * dy)) * nj + to_j) * nk + to_k)
                    )
        return pairs

    def local(
        inputs,
        attn_out,
        grad_out,
        grad_query,
        grad_key,
        grad_value,
        query_weight,
        key_weight,
        value_weight,
    ):
        i, j, k = lax.axis_index("ia"), lax.axis_index("ja"), lax.axis_index("ka")
        tok, width = inputs.shape[1], inputs.shape[2]
        feat = grad_query.shape[2] // per
        grads = (grad_query, grad_key, grad_value)

        live, before = {}, {}

        def send(stream, after=(), **values):
            earlier = before.get(stream, []) + [name for name in after if name in live]
            names = list(values)
            out = lax.optimization_barrier(
                tuple(values[name] for name in names) + tuple(live[name] for name in earlier)
            )
            live.update(zip(earlier, out[len(names) :]))
            before[stream] = names
            return out[: len(names)]

        def along_x(name, value, after=()):
            (value,) = send("x", after, **{name: value})
            live[name] = lax.ppermute(value, "ia", swap_x)

        def along_y(name, value, after=()):
            (value,) = send("y", after, **{name: value})
            live[name] = lax.ppermute(value, "ia", swap_y)

        def along_z(name, to_right, to_left, after=()):
            to_right, to_left = send("z", after, **{name + "_r": to_right, name + "_l": to_left})
            live[name + "_r"] = lax.ppermute(to_right, "ja", right)
            live[name + "_l"] = lax.ppermute(to_left, "ja", left)

        def keep(name, value, *start):
            live[name] = lax.dynamic_update_slice(live[name], value, start)

        def slot_of(source):
            return jnp.where(
                source == j, 0, jnp.where(source > j, source - j, nj - 1 - source)
            )

        deals = [(step, dy) for dy in range(2) for step in range(per)]

        def deal_piece(step, dy):
            chunk = (j + step) % per
            return jnp.concatenate(
                [
                    jnp.concatenate(
                        [
                            lax.dynamic_slice(
                                grad, (i ^ (2 * dy) ^ dx, 0, chunk * feat), (1, tok, feat)
                            ).reshape(tok, feat)
                            for grad in grads
                        ],
                        axis=1,
                    )
                    for dx in range(2)
                ],
                axis=0,
            )

        def deal(index):
            name = f"dealt{index}"
            (piece,) = send("deal", **{name: deal_piece(*deals[index])})
            live[name] = lax.ppermute(piece, ("ia", "ja", "ka"), deal_pairs(*deals[index]))

        def share(indices):
            if len(indices) == 0:
                return
            pieces = [live[f"dealt{index}"].reshape(2, 1, tok, 3 * feat) for index in indices]
            pieces = jnp.concatenate(pieces, axis=1)
            for hop in range(nk):
                for place_in, index in enumerate(indices):
                    step, dy = deals[index]
                    source = per * ((k - hop) % nk) + (j % per - step) % per
                    piece = pieces[:, place_in : place_in + 1]
                    keep("g", piece, 0, slot_of(source), 0, dy * 3 * feat)
                if hop < nk - 1:
                    pieces = lax.ppermute(pieces, "ka", core_ring)

        rows = inputs.reshape(tok, width)
        go_own = grad_out.reshape(tok, width)
        high = max(tok, feat)

        def fill(block):
            return jnp.pad(block, ((0, high - block.shape[0]), (0, 0)))

        along_z("line1", fill(rows), fill(rows))
        along_y("go2", go_own)
        along_x("go1", go_own)
        deal(0)
        along_y("wq", query_weight)
        along_x("go3", live["go2"])
        (mine,) = send("own", ("dealt0",), swap0=rows)
        live["swap0"] = lax.ppermute(mine, "ia", swap_x)
        deal(1)
        along_y("wk", key_weight)
        along_y("wv", value_weight)

        part = jnp.concatenate(
            [lax.dynamic_index_in_dim(attn_out, i ^ r, 0, keepdims=False) for r in range(ni)], axis=0
        )
        parts = list(send("attn", ("go1",), attn=part))
        go = jnp.concatenate((go_own, live["go1"], live["go2"], live["go3"]), axis=0)
        for _ in range(nk - 1):
            parts.append(lax.ppermute(parts[-1], "ka", core_ring))
        output_terms = dot_rows(jnp.concatenate(parts, axis=1), go)

        def output_chunk(dest):
            start = (((k - dest // per) % nk) * per + dest % per) * feat
            return lax.dynamic_slice(output_terms, (start, 0), (feat, width))

        live["g"] = jnp.zeros((2, nj, tok, 6 * feat), BF16)
        live["x"] = jnp.zeros((2 * nj * tok, width), BF16)
        keep("x", rows, 0, 0)
        come = {"r": [], "l": []}
        for step in range(1, nj + 1):
            for side in "rl":
                come[side].append(f"line{step}_{side}")
            if step < nj:
                part_r = output_chunk(jnp.minimum(nj - step + j, nj - 1))
                part_l = output_chunk(jnp.maximum(step + j - nj, 0))
                part_r = fill(jnp.where(j < step, part_r, 0.0))
                part_l = fill(jnp.where(j >= nj - step, part_l, 0.0))
                to_right = (live[f"line{step}_r"].astype(F32) + part_r).astype(BF16)
                to_left = (live[f"line{step}_l"].astype(F32) + part_l).astype(BF16)
                block = live[f"line{step}_l"]
                for near in range(1, step + 1):
                    block = jnp.where(j == nj - 1 - step + near, live[f"line{near}_r"], block)
                block = block[:tok]
                after = {1: ("dealt1",), 2: ("dealt3",), nj - 1: (f"swap{step}",)}
                if step < nj - 1:
                    along_z(f"line{step + 1}", to_right, to_left, after.get(step, ()))
                along_x(f"swap{step}", block, {2: ("swap0", "wk"), 3: ("wv",)}.get(step, ()))
                if step == nj - 1:
                    along_z(f"line{step + 1}", to_right, to_left, after[step])
                keep("x", block, step * tok, 0)
                if step > 1:
                    keep("x", live[f"swap{step - 1}"], (nj + step - 1) * tok, 0)
            if step == 1:
                for index in range(2, len(deals)):
                    deal(index)
            if step == 2:
                share(range(0, min(2, len(deals))))
        share(range(2, len(deals)))
        keep("x", live["swap0"], nj * tok, 0)
        w = jnp.concatenate(
            (query_weight, key_weight, value_weight, live["wq"], live["wk"], live["wv"]), axis=1
        )

        place = ring_place(j, nj)

        def chunk(bank, step):
            dest = ring_device((place - step) % nj, nj)
            part = lax.dynamic_index_in_dim(live["g"][bank], slot_of(dest), 0, keepdims=False)
            return dot_cols(part, w)

        def weight_term(w, count, first=0, end=2 * nj * tok):
            part = live["g"].reshape(2 * nj * tok, 6 * feat)
            return dot_rows(live["x"][first:end], part[first:end, w * feat : (w + count) * feat])

        last = (2 * nj - 1) * tok
        pair = lax.optimization_barrier(weight_term(3, 2, 0, last))
        along_x("other1", chunk(1, 1).astype(BF16))
        keep("x", live[f"swap{nj - 1}"], last, 0)
        along_y("pair", (pair + weight_term(3, 2, last)).astype(BF16), ("other1",))
        for step in range(2, nj + 1):
            along_x(
                f"other{step}", chunk(1, step).astype(BF16), ("pair",) if step == nj else ()
            )
            term = chunk(0, step - 1) + live[f"other{step - 1}"].astype(F32)
            if step > 2:
                term = lax.optimization_barrier(term) + live[f"sum{step - 2}"].astype(F32)
            (term,) = send("sum", **{f"sum{step - 1}": term.astype(BF16)})
            live[f"sum{step - 1}"] = lax.ppermute(term, "ja", ring)
        along_y("value", weight_term(5, 1).astype(BF16))
        grad_inputs = chunk(0, nj) + live[f"other{nj}"].astype(F32)
        grad_inputs = lax.optimization_barrier(grad_inputs) + live[f"sum{nj - 1}"].astype(F32)
        grad_inputs = grad_inputs.astype(BF16).reshape(inputs.shape)
        from_ends = live[f"line{nj}_r"].astype(F32) + live[f"line{nj}_l"].astype(F32)
        output_weight_grad = output_chunk(j) + from_ends[:feat]
        weight_grads = (
            weight_term(0, 1) + live["pair"][:, :feat].astype(F32),
            weight_term(1, 1) + live["pair"][:, feat:].astype(F32),
            weight_term(2, 1) + live["value"].astype(F32),
        )
        return (grad_inputs, *weight_grads, output_weight_grad)

    return local


def solution(mesh):
    return jax.shard_map(
        build(mesh),
        mesh=mesh,
        in_specs=(
            P("ia", "ja", "ka"),
            P(None, "ja", ("ia", "ka")),
            P("ia", "ja", "ka"),
            P(None, "ja", ("ia", "ka")),
            P(None, "ja", ("ia", "ka")),
            P(None, "ja", ("ia", "ka")),
            P("ka", ("ia", "ja")),
            P("ka", ("ia", "ja")),
            P("ka", ("ia", "ja")),
        ),
        out_specs=(
            P("ia", "ja", "ka"),
            P("ka", ("ia", "ja")),
            P("ka", ("ia", "ja")),
            P("ka", ("ia", "ja")),
            P(("ia", "ja"), "ka"),
        ),
        check_vma=False,
    )
```

```python
import jax
import jax.numpy as jnp
from jax import lax
from jax.sharding import PartitionSpec as P

BF16 = jnp.bfloat16
F32 = jnp.float32


def ring_place(j, n):
    return jnp.where(j % 2 == 1, (j + 1) // 2, (n - j // 2) % n)


def ring_device(place, n):
    return jnp.where(
        place == 0, 0, jnp.where(place <= n // 2, 2 * place - 1, 2 * (n - place))
    )


def ring_pairs(n):
    order = [0] + list(range(1, n, 2)) + list(range(n - 2, 0, -2))
    return [(order[p], order[(p + 1) % n]) for p in range(n)]


def dot_rows(a, b):
    return lax.dot_general(a, b, (((0,), (0,)), ((), ())), preferred_element_type=F32)


def dot_cols(a, b):
    return lax.dot_general(a, b, (((1,), (1,)), ((), ())), preferred_element_type=F32)


def build(mesh):
    ni, nj, nk = mesh.shape["ia"], mesh.shape["ja"], mesh.shape["ka"]
    assert ni == 4 and nj >= 4 and nj % nk == 0
    per = nj // nk
    swap_x = [(i, i ^ 1) for i in range(ni)]
    swap_y = [(i, i ^ 2) for i in range(ni)]
    right = [(j, j + 1) for j in range(nj - 1)]
    left = [(j + 1, j) for j in range(nj - 1)]
    ring = ring_pairs(nj)
    core_ring = [(k, (k + 1) % nk) for k in range(nk)]

    def deal_pairs(step, dy):
        pairs = []
        for i in range(ni):
            for j in range(nj):
                for k in range(nk):
                    to_j, to_k = per * k + (j + step) % per, j // per
                    pairs.append(
                        ((i * nj + j) * nk + k, ((i ^ (2 * dy)) * nj + to_j) * nk + to_k)
                    )
        return pairs

    def local(
        inputs,
        attn_out,
        grad_out,
        grad_query,
        grad_key,
        grad_value,
        query_weight,
        key_weight,
        value_weight,
    ):
        i, j, k = lax.axis_index("ia"), lax.axis_index("ja"), lax.axis_index("ka")
        tok, width = inputs.shape[1], inputs.shape[2]
        feat = grad_query.shape[2] // per
        grads = (grad_query, grad_key, grad_value)

        live, before = {}, {}

        def send(stream, after=(), **values):
            earlier = before.get(stream, []) + [name for name in after if name in live]
            names = list(values)
            out = lax.optimization_barrier(
                tuple(values[name] for name in names) + tuple(live[name] for name in earlier)
            )
            live.update(zip(earlier, out[len(names) :]))
            before[stream] = names
            return out[: len(names)]

        def along_x(name, value, after=()):
            (value,) = send("x", after, **{name: value})
            live[name] = lax.ppermute(value, "ia", swap_x)

        def along_y(name, value, after=()):
            (value,) = send("y", after, **{name: value})
            live[name] = lax.ppermute(value, "ia", swap_y)

        def along_z(name, to_right, to_left, after=()):
            to_right, to_left = send("z", after, **{name + "_r": to_right, name + "_l": to_left})
            live[name + "_r"] = lax.ppermute(to_right, "ja", right)
            live[name + "_l"] = lax.ppermute(to_left, "ja", left)

        def keep(name, value, *start):
            live[name] = lax.dynamic_update_slice(live[name], value, start)

        def slot_of(source):
            return jnp.where(
                source == j, 0, jnp.where(source > j, source - j, nj - 1 - source)
            )

        deals = [(step, dy) for dy in range(2) for step in range(per)]

        def deal_piece(step, dy):
            chunk = (j + step) % per
            return jnp.concatenate(
                [
                    jnp.concatenate(
                        [
                            lax.dynamic_slice(
                                grad, (i ^ (2 * dy) ^ dx, 0, chunk * feat), (1, tok, feat)
                            ).reshape(tok, feat)
                            for grad in grads
                        ],
                        axis=1,
                    )
                    for dx in range(2)
                ],
                axis=0,
            )

        def deal(index):
            name = f"dealt{index}"
            (piece,) = send("deal", **{name: deal_piece(*deals[index])})
            live[name] = lax.ppermute(piece, ("ia", "ja", "ka"), deal_pairs(*deals[index]))

        def share(indices):
            if len(indices) == 0:
                return
            pieces = [live[f"dealt{index}"].reshape(2, 1, tok, 3 * feat) for index in indices]
            pieces = jnp.concatenate(pieces, axis=1)
            for hop in range(nk):
                for place_in, index in enumerate(indices):
                    step, dy = deals[index]
                    source = per * ((k - hop) % nk) + (j % per - step) % per
                    piece = pieces[:, place_in : place_in + 1]
                    keep("g", piece, 0, slot_of(source), 0, dy * 3 * feat)
                if hop < nk - 1:
                    pieces = lax.ppermute(pieces, "ka", core_ring)

        rows = inputs.reshape(tok, width)
        go_own = grad_out.reshape(tok, width)
        high = max(tok, feat)

        def fill(block):
            return jnp.pad(block, ((0, high - block.shape[0]), (0, 0)))

        along_z("line1", fill(rows), fill(rows))
        along_y("go2", go_own)
        along_x("go1", go_own)
        deal(0)
        along_y("wq", query_weight)
        along_x("go3", live["go2"])
        (mine,) = send("own", ("dealt0",), swap0=rows)
        live["swap0"] = lax.ppermute(mine, "ia", swap_x)
        deal(1)
        along_y("wk", key_weight)
        along_y("wv", value_weight)

        part = jnp.concatenate(
            [lax.dynamic_index_in_dim(attn_out, i ^ r, 0, keepdims=False) for r in range(ni)], axis=0
        )
        parts = list(send("attn", ("go1",), attn=part))
        go = jnp.concatenate((go_own, live["go1"], live["go2"], live["go3"]), axis=0)
        for _ in range(nk - 1):
            parts.append(lax.ppermute(parts[-1], "ka", core_ring))
        output_terms = dot_rows(jnp.concatenate(parts, axis=1), go)

        def output_chunk(dest):
            start = (((k - dest // per) % nk) * per + dest % per) * feat
            return lax.dynamic_slice(output_terms, (start, 0), (feat, width))

        live["g"] = jnp.zeros((2, nj, tok, 6 * feat), BF16)
        live["x"] = jnp.zeros((2 * nj * tok, width), BF16)
        keep("x", rows, 0, 0)
        come = {"r": [], "l": []}
        for step in range(1, nj + 1):
            for side in "rl":
                come[side].append(f"line{step}_{side}")
            if step < nj:
                part_r = output_chunk(jnp.minimum(nj - step + j, nj - 1))
                part_l = output_chunk(jnp.maximum(step + j - nj, 0))
                part_r = fill(jnp.where(j < step, part_r, 0.0))
                part_l = fill(jnp.where(j >= nj - step, part_l, 0.0))
                to_right = (live[f"line{step}_r"].astype(F32) + part_r).astype(BF16)
                to_left = (live[f"line{step}_l"].astype(F32) + part_l).astype(BF16)
                block = live[f"line{step}_l"]
                for near in range(1, step + 1):
                    block = jnp.where(j == nj - 1 - step + near, live[f"line{near}_r"], block)
                block = block[:tok]
                after = {1: ("dealt1",), 2: ("dealt3",), nj - 1: (f"swap{step}",)}
                if step < nj - 1:
                    along_z(f"line{step + 1}", to_right, to_left, after.get(step, ()))
                along_x(f"swap{step}", block, {2: ("swap0", "wk"), 3: ("wv",)}.get(step, ()))
                if step == nj - 1:
                    along_z(f"line{step + 1}", to_right, to_left, after[step])
                keep("x", block, step * tok, 0)
                if step > 1:
                    keep("x", live[f"swap{step - 1}"], (nj + step - 1) * tok, 0)
            if step == 1:
                for index in range(2, len(deals)):
                    deal(index)
            if step == 2:
                share(range(0, min(2, len(deals))))
        share(range(2, len(deals)))
        keep("x", live["swap0"], nj * tok, 0)
        w = jnp.concatenate(
            (query_weight, key_weight, value_weight, live["wq"], live["wk"], live["wv"]), axis=1
        )

        place = ring_place(j, nj)

        def chunk(bank, step):
            dest = ring_device((place - step) % nj, nj)
            part = lax.dynamic_index_in_dim(live["g"][bank], slot_of(dest), 0, keepdims=False)
            return dot_cols(part, w)

        def weight_term(w, count):
            part = live["g"].reshape(2 * nj * tok, 6 * feat)
            return dot_rows(live["x"], part[:, w * feat : (w + count) * feat])

        def hold(name):
            live["g"], live[name] = lax.optimization_barrier((live["g"], live[name]))

        other = chunk(1, 1).astype(BF16)
        own = lax.optimization_barrier(chunk(0, 1))
        (other,) = send("first", (f"swap{nj - 2}",), other1=other)
        live["other1"] = lax.ppermute(other, "ia", swap_x)
        hold(f"swap{nj - 1}")
        keep("x", live[f"swap{nj - 1}"], (2 * nj - 1) * tok, 0)
        along_y("pair", weight_term(3, 2).astype(BF16), ("other1",))
        for step in range(2, nj + 1):
            if step > 2:
                hold(f"other{step - 2}")
            after = {2: ("other1",), nj: ("pair",)}
            along_x(f"other{step}", chunk(1, step).astype(BF16), after.get(step, ()))
            term = own + live[f"other{step - 1}"].astype(F32)
            own = lax.optimization_barrier(chunk(0, step))
            if step > 2:
                term = lax.optimization_barrier(term) + live[f"sum{step - 2}"].astype(F32)
            (term,) = send("sum", **{f"sum{step - 1}": term.astype(BF16)})
            live[f"sum{step - 1}"] = lax.ppermute(term, "ja", ring)
        along_y("value", weight_term(5, 1).astype(BF16))
        grad_inputs = own + live[f"other{nj}"].astype(F32)
        grad_inputs = lax.optimization_barrier(grad_inputs) + live[f"sum{nj - 1}"].astype(F32)
        grad_inputs = grad_inputs.astype(BF16).reshape(inputs.shape)
        from_ends = live[f"line{nj}_r"].astype(F32) + live[f"line{nj}_l"].astype(F32)
        output_weight_grad = output_chunk(j) + from_ends[:feat]
        weight_grads = (
            weight_term(0, 1) + live["pair"][:, :feat].astype(F32),
            weight_term(1, 1) + live["pair"][:, feat:].astype(F32),
            weight_term(2, 1) + live["value"].astype(F32),
        )
        return (grad_inputs, *weight_grads, output_weight_grad)

    return local


def solution(mesh):
    return jax.shard_map(
        build(mesh),
        mesh=mesh,
        in_specs=(
            P("ia", "ja", "ka"),
            P(None, "ja", ("ia", "ka")),
            P("ia", "ja", "ka"),
            P(None, "ja", ("ia", "ka")),
            P(None, "ja", ("ia", "ka")),
            P(None, "ja", ("ia", "ka")),
            P("ka", ("ia", "ja")),
            P("ka", ("ia", "ja")),
            P("ka", ("ia", "ja")),
        ),
        out_specs=(
            P("ia", "ja", "ka"),
            P("ka", ("ia", "ja")),
            P("ka", ("ia", "ja")),
            P("ka", ("ia", "ja")),
            P(("ia", "ja"), "ka"),
        ),
        check_vma=False,
    )
```

```python
import jax
import jax.numpy as jnp
from jax import lax
from jax.sharding import PartitionSpec as P

BF16 = jnp.bfloat16
F32 = jnp.float32


def ring_place(j, n):
    return jnp.where(j % 2 == 1, (j + 1) // 2, (n - j // 2) % n)


def ring_device(place, n):
    return jnp.where(
        place == 0, 0, jnp.where(place <= n // 2, 2 * place - 1, 2 * (n - place))
    )


def ring_pairs(n):
    order = [0] + list(range(1, n, 2)) + list(range(n - 2, 0, -2))
    return [(order[p], order[(p + 1) % n]) for p in range(n)]


def dot_rows(a, b):
    return lax.dot_general(a, b, (((0,), (0,)), ((), ())), preferred_element_type=F32)


def dot_cols(a, b):
    return lax.dot_general(a, b, (((1,), (1,)), ((), ())), preferred_element_type=F32)


def build(mesh):
    ni, nj, nk = mesh.shape["ia"], mesh.shape["ja"], mesh.shape["ka"]
    assert ni == 4 and nj >= 4 and nj % nk == 0
    per = nj // nk
    swap_x = [(i, i ^ 1) for i in range(ni)]
    swap_y = [(i, i ^ 2) for i in range(ni)]
    right = [(j, j + 1) for j in range(nj - 1)]
    left = [(j + 1, j) for j in range(nj - 1)]
    ring = ring_pairs(nj)
    core_ring = [(k, (k + 1) % nk) for k in range(nk)]

    def deal_pairs(step, dy):
        pairs = []
        for i in range(ni):
            for j in range(nj):
                for k in range(nk):
                    to_j, to_k = per * k + (j + step) % per, j // per
                    pairs.append(
                        ((i * nj + j) * nk + k, ((i ^ (2 * dy)) * nj + to_j) * nk + to_k)
                    )
        return pairs

    def local(
        inputs,
        attn_out,
        grad_out,
        grad_query,
        grad_key,
        grad_value,
        query_weight,
        key_weight,
        value_weight,
    ):
        i, j, k = lax.axis_index("ia"), lax.axis_index("ja"), lax.axis_index("ka")
        tok, width = inputs.shape[1], inputs.shape[2]
        feat = grad_query.shape[2] // per
        grads = (grad_query, grad_key, grad_value)

        live, before = {}, {}

        def send(stream, after=(), **values):
            earlier = before.get(stream, []) + [name for name in after if name in live]
            names = list(values)
            out = lax.optimization_barrier(
                tuple(values[name] for name in names) + tuple(live[name] for name in earlier)
            )
            live.update(zip(earlier, out[len(names) :]))
            before[stream] = names
            return out[: len(names)]

        def along_x(name, value, after=()):
            (value,) = send("x", after, **{name: value})
            live[name] = lax.ppermute(value, "ia", swap_x)

        def along_y(name, value, after=()):
            (value,) = send("y", after, **{name: value})
            live[name] = lax.ppermute(value, "ia", swap_y)

        def along_z(name, to_right, to_left, after=()):
            to_right, to_left = send("z", after, **{name + "_r": to_right, name + "_l": to_left})
            live[name + "_r"] = lax.ppermute(to_right, "ja", right)
            live[name + "_l"] = lax.ppermute(to_left, "ja", left)

        def keep(name, value, *start):
            live[name] = lax.dynamic_update_slice(live[name], value, start)

        def slot_of(source):
            return jnp.where(
                source == j, 0, jnp.where(source > j, source - j, nj - 1 - source)
            )

        deals = [(step, dy) for dy in range(2) for step in range(per)]

        def deal_piece(step, dy):
            chunk = (j + step) % per
            return jnp.concatenate(
                [
                    jnp.concatenate(
                        [
                            lax.dynamic_slice(
                                grad, (i ^ (2 * dy) ^ dx, 0, chunk * feat), (1, tok, feat)
                            ).reshape(tok, feat)
                            for grad in grads
                        ],
                        axis=1,
                    )
                    for dx in range(2)
                ],
                axis=0,
            )

        def deal(index):
            name = f"dealt{index}"
            (piece,) = send("deal", **{name: deal_piece(*deals[index])})
            live[name] = lax.ppermute(piece, ("ia", "ja", "ka"), deal_pairs(*deals[index]))

        def share(indices):
            if len(indices) == 0:
                return
            pieces = [live[f"dealt{index}"].reshape(2, 1, tok, 3 * feat) for index in indices]
            pieces = jnp.concatenate(pieces, axis=1)
            for hop in range(nk):
                for place_in, index in enumerate(indices):
                    step, dy = deals[index]
                    source = per * ((k - hop) % nk) + (j % per - step) % per
                    piece = pieces[:, place_in : place_in + 1]
                    keep("g", piece, 0, slot_of(source), 0, dy * 3 * feat)
                if hop < nk - 1:
                    pieces = lax.ppermute(pieces, "ka", core_ring)

        rows = inputs.reshape(tok, width)
        go_own = grad_out.reshape(tok, width)
        high = max(tok, feat)

        def fill(block):
            return jnp.pad(block, ((0, high - block.shape[0]), (0, 0)))

        along_z("line1", fill(rows), fill(rows))
        along_y("go2", go_own)
        along_x("go1", go_own)
        deal(0)
        along_y("wq", query_weight)
        along_x("go3", live["go2"])
        (mine,) = send("own", ("dealt0",), swap0=rows)
        live["swap0"] = lax.ppermute(mine, "ia", swap_x)
        deal(1)
        along_y("wk", key_weight)
        along_y("wv", value_weight)

        part = jnp.concatenate(
            [lax.dynamic_index_in_dim(attn_out, i ^ r, 0, keepdims=False) for r in range(ni)], axis=0
        )
        parts = list(send("attn", ("go1",), attn=part))
        go = jnp.concatenate((go_own, live["go1"], live["go2"], live["go3"]), axis=0)
        for _ in range(nk - 1):
            parts.append(lax.ppermute(parts[-1], "ka", core_ring))
        output_terms = dot_rows(jnp.concatenate(parts, axis=1), go)

        def output_chunk(dest):
            start = (((k - dest // per) % nk) * per + dest % per) * feat
            return lax.dynamic_slice(output_terms, (start, 0), (feat, width))

        live["g"] = jnp.zeros((2, nj, tok, 6 * feat), BF16)
        live["x"] = jnp.zeros((2 * nj * tok, width), BF16)
        keep("x", rows, 0, 0)
        come = {"r": [], "l": []}
        for step in range(1, nj + 1):
            for side in "rl":
                come[side].append(f"line{step}_{side}")
            if step < nj:
                part_r = output_chunk(jnp.minimum(nj - step + j, nj - 1))
                part_l = output_chunk(jnp.maximum(step + j - nj, 0))
                part_r = fill(jnp.where(j < step, part_r, 0.0))
                part_l = fill(jnp.where(j >= nj - step, part_l, 0.0))
                to_right = (live[f"line{step}_r"].astype(F32) + part_r).astype(BF16)
                to_left = (live[f"line{step}_l"].astype(F32) + part_l).astype(BF16)
                block = live[f"line{step}_l"]
                for near in range(1, step + 1):
                    block = jnp.where(j == nj - 1 - step + near, live[f"line{near}_r"], block)
                block = block[:tok]
                after = {1: ("dealt1",), 2: ("dealt3",), nj - 1: (f"swap{step - 1}",)}
                if step < nj - 1:
                    along_z(f"line{step + 1}", to_right, to_left, after.get(step, ()))
                along_x(f"swap{step}", block, {2: ("swap0", "wk"), 3: ("wv",)}.get(step, ()))
                if step == nj - 1:
                    along_z(f"line{step + 1}", to_right, to_left, after[step])
                keep("x", block, step * tok, 0)
                if step > 1:
                    keep("x", live[f"swap{step - 1}"], (nj + step - 1) * tok, 0)
            if step == 1:
                for index in range(2, len(deals)):
                    deal(index)
            if step == 2:
                share(range(0, min(2, len(deals))))
        share(range(2, len(deals)))
        keep("x", live["swap0"], nj * tok, 0)
        w = jnp.concatenate(
            (query_weight, key_weight, value_weight, live["wq"], live["wk"], live["wv"]), axis=1
        )

        place = ring_place(j, nj)

        def chunk(bank, step):
            dest = ring_device((place - step) % nj, nj)
            part = lax.dynamic_index_in_dim(live["g"][bank], slot_of(dest), 0, keepdims=False)
            return dot_cols(part, w)

        def weight_term(w, count):
            part = live["g"].reshape(2 * nj * tok, 6 * feat)
            return dot_rows(live["x"], part[:, w * feat : (w + count) * feat])

        def hold(*names):
            names = ("g",) + names
            out = lax.optimization_barrier(tuple(live[name] for name in names))
            live.update(zip(names, out))

        other = chunk(1, 1).astype(BF16)
        own = lax.optimization_barrier(chunk(0, 1))
        (other,) = send("first", (f"swap{nj - 2}",), other1=other)
        live["other1"] = lax.ppermute(other, "ia", swap_x)
        hold(f"swap{nj - 1}", f"line{nj}_r", f"line{nj}_l")
        keep("x", live[f"swap{nj - 1}"], (2 * nj - 1) * tok, 0)
        along_y("pair", weight_term(3, 2).astype(BF16))
        for step in range(2, nj + 1):
            if step > 2:
                hold(f"other{step - 2}")
            after = {2: ("other1",), nj: ("pair",)}
            along_x(f"other{step}", chunk(1, step).astype(BF16), after.get(step, ()))
            term = own + live[f"other{step - 1}"].astype(F32)
            own = lax.optimization_barrier(chunk(0, step))
            if step > 2:
                term = lax.optimization_barrier(term) + live[f"sum{step - 2}"].astype(F32)
            (term,) = send("sum", **{f"sum{step - 1}": term.astype(BF16)})
            live[f"sum{step - 1}"] = lax.ppermute(term, "ja", ring)
        along_y("value", weight_term(5, 1).astype(BF16))
        value_own = lax.optimization_barrier(weight_term(2, 1))
        grad_inputs = own + live[f"other{nj}"].astype(F32)
        grad_inputs = lax.optimization_barrier(grad_inputs) + live[f"sum{nj - 1}"].astype(F32)
        grad_inputs = grad_inputs.astype(BF16).reshape(inputs.shape)
        from_ends = live[f"line{nj}_r"].astype(F32) + live[f"line{nj}_l"].astype(F32)
        output_weight_grad = output_chunk(j) + from_ends[:feat]
        weight_grads = (
            weight_term(0, 1) + live["pair"][:, :feat].astype(F32),
            weight_term(1, 1) + live["pair"][:, feat:].astype(F32),
            value_own + live["value"].astype(F32),
        )
        return (grad_inputs, *weight_grads, output_weight_grad)

    return local


def solution(mesh):
    return jax.shard_map(
        build(mesh),
        mesh=mesh,
        in_specs=(
            P("ia", "ja", "ka"),
            P(None, "ja", ("ia", "ka")),
            P("ia", "ja", "ka"),
            P(None, "ja", ("ia", "ka")),
            P(None, "ja", ("ia", "ka")),
            P(None, "ja", ("ia", "ka")),
            P("ka", ("ia", "ja")),
            P("ka", ("ia", "ja")),
            P("ka", ("ia", "ja")),
        ),
        out_specs=(
            P("ia", "ja", "ka"),
            P("ka", ("ia", "ja")),
            P("ka", ("ia", "ja")),
            P("ka", ("ia", "ja")),
            P(("ia", "ja"), "ka"),
        ),
        check_vma=False,
    )
```

```python
import jax
import jax.numpy as jnp
from jax import lax
from jax.sharding import PartitionSpec as P

BF16 = jnp.bfloat16
F32 = jnp.float32


def ring_place(j, n):
    return jnp.where(j % 2 == 1, (j + 1) // 2, (n - j // 2) % n)


def ring_device(place, n):
    return jnp.where(
        place == 0, 0, jnp.where(place <= n // 2, 2 * place - 1, 2 * (n - place))
    )


def ring_pairs(n):
    order = [0] + list(range(1, n, 2)) + list(range(n - 2, 0, -2))
    return [(order[p], order[(p + 1) % n]) for p in range(n)]


def dot_rows(a, b):
    return lax.dot_general(a, b, (((0,), (0,)), ((), ())), preferred_element_type=F32)


def dot_cols(a, b):
    return lax.dot_general(a, b, (((1,), (1,)), ((), ())), preferred_element_type=F32)


def build(mesh):
    ni, nj, nk = mesh.shape["ia"], mesh.shape["ja"], mesh.shape["ka"]
    assert ni == 4 and nj >= 4 and nj % nk == 0
    per = nj // nk
    swap_x = [(i, i ^ 1) for i in range(ni)]
    swap_y = [(i, i ^ 2) for i in range(ni)]
    right = [(j, j + 1) for j in range(nj - 1)]
    left = [(j + 1, j) for j in range(nj - 1)]
    ring = ring_pairs(nj)
    core_ring = [(k, (k + 1) % nk) for k in range(nk)]

    def deal_pairs(step, dy):
        pairs = []
        for i in range(ni):
            for j in range(nj):
                for k in range(nk):
                    to_j, to_k = per * k + (j + step) % per, j // per
                    pairs.append(
                        ((i * nj + j) * nk + k, ((i ^ (2 * dy)) * nj + to_j) * nk + to_k)
                    )
        return pairs

    def local(
        inputs,
        attn_out,
        grad_out,
        grad_query,
        grad_key,
        grad_value,
        query_weight,
        key_weight,
        value_weight,
    ):
        i, j, k = lax.axis_index("ia"), lax.axis_index("ja"), lax.axis_index("ka")
        tok, width = inputs.shape[1], inputs.shape[2]
        feat = grad_query.shape[2] // per
        grads = (grad_query, grad_key, grad_value)

        live, before = {}, {}

        def send(stream, after=(), **values):
            earlier = before.get(stream, []) + [name for name in after if name in live]
            names = list(values)
            out = lax.optimization_barrier(
                tuple(values[name] for name in names) + tuple(live[name] for name in earlier)
            )
            live.update(zip(earlier, out[len(names) :]))
            before[stream] = names
            return out[: len(names)]

        def along_x(name, value, after=()):
            (value,) = send("x", after, **{name: value})
            live[name] = lax.ppermute(value, "ia", swap_x)

        def along_y(name, value, after=()):
            (value,) = send("y", after, **{name: value})
            live[name] = lax.ppermute(value, "ia", swap_y)

        def along_z(name, to_right, to_left, after=()):
            to_right, to_left = send("z", after, **{name + "_r": to_right, name + "_l": to_left})
            live[name + "_r"] = lax.ppermute(to_right, "ja", right)
            live[name + "_l"] = lax.ppermute(to_left, "ja", left)

        def keep(name, value, *start):
            live[name] = lax.dynamic_update_slice(live[name], value, start)

        def slot_of(source):
            return jnp.where(
                source == j, 0, jnp.where(source > j, source - j, nj - 1 - source)
            )

        deals = [(step, dy) for dy in range(2) for step in range(per)]

        def deal_piece(step, dy):
            chunk = (j + step) % per
            return jnp.concatenate(
                [
                    jnp.concatenate(
                        [
                            lax.dynamic_slice(
                                grad, (i ^ (2 * dy) ^ dx, 0, chunk * feat), (1, tok, feat)
                            ).reshape(tok, feat)
                            for grad in grads
                        ],
                        axis=1,
                    )
                    for dx in range(2)
                ],
                axis=0,
            )

        def deal(index):
            name = f"dealt{index}"
            (piece,) = send("deal", **{name: deal_piece(*deals[index])})
            live[name] = lax.ppermute(piece, ("ia", "ja", "ka"), deal_pairs(*deals[index]))

        def share(indices):
            if len(indices) == 0:
                return
            pieces = [live[f"dealt{index}"].reshape(2, 1, tok, 3 * feat) for index in indices]
            pieces = jnp.concatenate(pieces, axis=1)
            for hop in range(nk):
                for place_in, index in enumerate(indices):
                    step, dy = deals[index]
                    source = per * ((k - hop) % nk) + (j % per - step) % per
                    piece = pieces[:, place_in : place_in + 1]
                    keep("g", piece, 0, slot_of(source), 0, dy * 3 * feat)
                if hop < nk - 1:
                    pieces = lax.ppermute(pieces, "ka", core_ring)

        rows = inputs.reshape(tok, width)
        go_own = grad_out.reshape(tok, width)
        high = max(tok, feat)

        def fill(block):
            return jnp.pad(block, ((0, high - block.shape[0]), (0, 0)))

        along_z("line1", fill(rows), fill(rows))
        along_y("go2", go_own)
        along_x("go1", go_own)
        deal(0)
        along_y("wq", query_weight)
        along_x("go3", live["go2"])
        (mine,) = send("own", ("dealt0",), swap0=rows)
        live["swap0"] = lax.ppermute(mine, "ia", swap_x)
        deal(1)
        along_y("wk", key_weight)
        along_y("wv", value_weight)

        part = jnp.concatenate(
            [lax.dynamic_index_in_dim(attn_out, i ^ r, 0, keepdims=False) for r in range(ni)], axis=0
        )
        parts = list(send("attn", ("go1",), attn=part))
        go = jnp.concatenate((go_own, live["go1"], live["go2"], live["go3"]), axis=0)
        for _ in range(nk - 1):
            parts.append(lax.ppermute(parts[-1], "ka", core_ring))
        output_terms = dot_rows(jnp.concatenate(parts, axis=1), go)

        def output_chunk(dest):
            start = (((k - dest // per) % nk) * per + dest % per) * feat
            return lax.dynamic_slice(output_terms, (start, 0), (feat, width))

        live["g"] = jnp.zeros((2, nj, tok, 6 * feat), BF16)
        live["x"] = jnp.zeros((2 * nj * tok, width), BF16)
        keep("x", rows, 0, 0)
        come = {"r": [], "l": []}
        for step in range(1, nj + 1):
            for side in "rl":
                come[side].append(f"line{step}_{side}")
            if step < nj:
                part_r = output_chunk(jnp.minimum(nj - step + j, nj - 1))
                part_l = output_chunk(jnp.maximum(step + j - nj, 0))
                part_r = fill(jnp.where(j < step, part_r, 0.0))
                part_l = fill(jnp.where(j >= nj - step, part_l, 0.0))
                to_right = (live[f"line{step}_r"].astype(F32) + part_r).astype(BF16)
                to_left = (live[f"line{step}_l"].astype(F32) + part_l).astype(BF16)
                block = live[f"line{step}_l"]
                for near in range(1, step + 1):
                    block = jnp.where(j == nj - 1 - step + near, live[f"line{near}_r"], block)
                block = block[:tok]
                after = {1: ("dealt1",), 2: ("dealt3",), nj - 1: (f"swap{step}",)}
                if step < nj - 1:
                    along_z(f"line{step + 1}", to_right, to_left, after.get(step, ()))
                along_x(f"swap{step}", block, {2: ("swap0", "wk"), 3: ("wv",)}.get(step, ()))
                if step == nj - 1:
                    along_z(f"line{step + 1}", to_right, to_left, after[step])
                keep("x", block, step * tok, 0)
                if step > 1:
                    keep("x", live[f"swap{step - 1}"], (nj + step - 1) * tok, 0)
            if step == 1:
                for index in range(2, len(deals)):
                    deal(index)
            if step == 2:
                share(range(0, min(2, len(deals))))
        share(range(2, len(deals)))
        keep("x", live["swap0"], nj * tok, 0)
        w = jnp.concatenate(
            (query_weight, key_weight, value_weight, live["wq"], live["wk"], live["wv"]), axis=1
        )

        place = ring_place(j, nj)

        def chunk(bank, step):
            dest = ring_device((place - step) % nj, nj)
            part = lax.dynamic_index_in_dim(live["g"][bank], slot_of(dest), 0, keepdims=False)
            return dot_cols(part, w)

        last = (2 * nj - 1) * tok

        def weight_term(w, count, first=0, end=2 * nj * tok):
            part = live["g"].reshape(2 * nj * tok, 6 * feat)
            return dot_rows(live["x"][first:end], part[first:end, w * feat : (w + count) * feat])

        def hold(name):
            live["g"], live[name] = lax.optimization_barrier((live["g"], live[name]))

        other = chunk(1, 1).astype(BF16)
        own = lax.optimization_barrier(chunk(0, 1))
        (other,) = send("first", (f"swap{nj - 2}",), other1=other)
        live["other1"] = lax.ppermute(other, "ia", swap_x)
        pair = lax.optimization_barrier(weight_term(3, 2, 0, last))
        hold(f"swap{nj - 1}")
        keep("x", live[f"swap{nj - 1}"], last, 0)
        along_y("pair", (pair + weight_term(3, 2, last)).astype(BF16))
        for step in range(2, nj + 1):
            if step > 2:
                hold(f"other{step - 2}")
            if step == nj:
                names = (f"line{nj}_r", f"line{nj}_l", f"other{nj - 1}")
                live.update(zip(names, lax.optimization_barrier(tuple(live[n] for n in names))))
            after = {2: ("other1",), nj: ("pair",)}
            along_x(f"other{step}", chunk(1, step).astype(BF16), after.get(step, ()))
            term = own + live[f"other{step - 1}"].astype(F32)
            own = lax.optimization_barrier(chunk(0, step))
            if step > 2:
                term = lax.optimization_barrier(term) + live[f"sum{step - 2}"].astype(F32)
            (term,) = send("sum", **{f"sum{step - 1}": term.astype(BF16)})
            live[f"sum{step - 1}"] = lax.ppermute(term, "ja", ring)
        along_y("value", weight_term(5, 1).astype(BF16))
        value_own = lax.optimization_barrier(weight_term(2, 1))
        grad_inputs = own + live[f"other{nj}"].astype(F32)
        grad_inputs = lax.optimization_barrier(grad_inputs) + live[f"sum{nj - 1}"].astype(F32)
        grad_inputs = grad_inputs.astype(BF16).reshape(inputs.shape)
        from_ends = live[f"line{nj}_r"].astype(F32) + live[f"line{nj}_l"].astype(F32)
        output_weight_grad = output_chunk(j) + from_ends[:feat]
        weight_grads = (
            weight_term(0, 1) + live["pair"][:, :feat].astype(F32),
            weight_term(1, 1) + live["pair"][:, feat:].astype(F32),
            value_own + live["value"].astype(F32),
        )
        return (grad_inputs, *weight_grads, output_weight_grad)

    return local


def solution(mesh):
    return jax.shard_map(
        build(mesh),
        mesh=mesh,
        in_specs=(
            P("ia", "ja", "ka"),
            P(None, "ja", ("ia", "ka")),
            P("ia", "ja", "ka"),
            P(None, "ja", ("ia", "ka")),
            P(None, "ja", ("ia", "ka")),
            P(None, "ja", ("ia", "ka")),
            P("ka", ("ia", "ja")),
            P("ka", ("ia", "ja")),
            P("ka", ("ia", "ja")),
        ),
        out_specs=(
            P("ia", "ja", "ka"),
            P("ka", ("ia", "ja")),
            P("ka", ("ia", "ja")),
            P("ka", ("ia", "ja")),
            P(("ia", "ja"), "ka"),
        ),
        check_vma=False,
    )
```

```python
import jax
import jax.numpy as jnp
from jax import lax
from jax.sharding import PartitionSpec as P

BF16 = jnp.bfloat16
F32 = jnp.float32


def ring_place(j, n):
    return jnp.where(j % 2 == 1, (j + 1) // 2, (n - j // 2) % n)


def ring_device(place, n):
    return jnp.where(
        place == 0, 0, jnp.where(place <= n // 2, 2 * place - 1, 2 * (n - place))
    )


def ring_pairs(n):
    order = [0] + list(range(1, n, 2)) + list(range(n - 2, 0, -2))
    return [(order[p], order[(p + 1) % n]) for p in range(n)]


def dot_rows(a, b):
    return lax.dot_general(a, b, (((0,), (0,)), ((), ())), preferred_element_type=F32)


def dot_cols(a, b):
    return lax.dot_general(a, b, (((1,), (1,)), ((), ())), preferred_element_type=F32)


def build(mesh):
    ni, nj, nk = mesh.shape["ia"], mesh.shape["ja"], mesh.shape["ka"]
    assert ni == 4 and nj >= 4 and nj % nk == 0
    per = nj // nk
    swap_x = [(i, i ^ 1) for i in range(ni)]
    swap_y = [(i, i ^ 2) for i in range(ni)]
    right = [(j, j + 1) for j in range(nj - 1)]
    left = [(j + 1, j) for j in range(nj - 1)]
    ring = ring_pairs(nj)
    core_ring = [(k, (k + 1) % nk) for k in range(nk)]

    def deal_pairs(step, dy):
        pairs = []
        for i in range(ni):
            for j in range(nj):
                for k in range(nk):
                    to_j, to_k = per * k + (j + step) % per, j // per
                    pairs.append(
                        ((i * nj + j) * nk + k, ((i ^ (2 * dy)) * nj + to_j) * nk + to_k)
                    )
        return pairs

    def local(
        inputs,
        attn_out,
        grad_out,
        grad_query,
        grad_key,
        grad_value,
        query_weight,
        key_weight,
        value_weight,
    ):
        i, j, k = lax.axis_index("ia"), lax.axis_index("ja"), lax.axis_index("ka")
        tok, width = inputs.shape[1], inputs.shape[2]
        feat = grad_query.shape[2] // per
        grads = (grad_query, grad_key, grad_value)

        live, before = {}, {}

        def send(stream, after=(), **values):
            earlier = before.get(stream, []) + [name for name in after if name in live]
            names = list(values)
            out = lax.optimization_barrier(
                tuple(values[name] for name in names) + tuple(live[name] for name in earlier)
            )
            live.update(zip(earlier, out[len(names) :]))
            before[stream] = names
            return out[: len(names)]

        def along_x(name, value, after=()):
            (value,) = send("x", after, **{name: value})
            live[name] = lax.ppermute(value, "ia", swap_x)

        def along_y(name, value, after=()):
            (value,) = send("y", after, **{name: value})
            live[name] = lax.ppermute(value, "ia", swap_y)

        def along_z(name, to_right, to_left, after=()):
            to_right, to_left = send("z", after, **{name + "_r": to_right, name + "_l": to_left})
            live[name + "_r"] = lax.ppermute(to_right, "ja", right)
            live[name + "_l"] = lax.ppermute(to_left, "ja", left)

        def keep(name, value, *start):
            live[name] = lax.dynamic_update_slice(live[name], value, start)

        def slot_of(source):
            return jnp.where(
                source == j, 0, jnp.where(source > j, source - j, nj - 1 - source)
            )

        deals = [(step, dy) for dy in range(2) for step in range(per)]

        def deal_piece(step, dy):
            chunk = (j + step) % per
            return jnp.concatenate(
                [
                    jnp.concatenate(
                        [
                            lax.dynamic_slice(
                                grad, (i ^ (2 * dy) ^ dx, 0, chunk * feat), (1, tok, feat)
                            ).reshape(tok, feat)
                            for grad in grads
                        ],
                        axis=1,
                    )
                    for dx in range(2)
                ],
                axis=0,
            )

        def deal(index):
            name = f"dealt{index}"
            if index < 2:
                before.pop("deal", None)
            (piece,) = send("deal", **{name: deal_piece(*deals[index])})
            live[name] = lax.ppermute(piece, ("ia", "ja", "ka"), deal_pairs(*deals[index]))

        def share(indices):
            if len(indices) == 0:
                return
            pieces = [live[f"dealt{index}"].reshape(2, 1, tok, 3 * feat) for index in indices]
            pieces = jnp.concatenate(pieces, axis=1)
            for hop in range(nk):
                for place_in, index in enumerate(indices):
                    step, dy = deals[index]
                    source = per * ((k - hop) % nk) + (j % per - step) % per
                    piece = pieces[:, place_in : place_in + 1]
                    keep("g", piece, 0, slot_of(source), 0, dy * 3 * feat)
                if hop < nk - 1:
                    pieces = lax.ppermute(pieces, "ka", core_ring)

        rows = inputs.reshape(tok, width)
        go_own = grad_out.reshape(tok, width)
        high = max(tok, feat)

        def fill(block):
            return jnp.pad(block, ((0, high - block.shape[0]), (0, 0)))

        along_z("line1", fill(rows), fill(rows))
        along_y("go2", go_own)
        along_x("go1", go_own)
        deal(0)
        along_y("wq", query_weight)
        along_x("go3", live["go2"])
        (mine,) = send("own", ("dealt0",), swap0=rows)
        live["swap0"] = lax.ppermute(mine, "ia", swap_x)
        deal(1)
        along_y("wk", key_weight)
        along_y("wv", value_weight)

        part = jnp.concatenate(
            [lax.dynamic_index_in_dim(attn_out, i ^ r, 0, keepdims=False) for r in range(ni)], axis=0
        )
        parts = list(send("attn", ("go1",), attn=part))
        go = jnp.concatenate((go_own, live["go1"], live["go2"], live["go3"]), axis=0)
        for _ in range(nk - 1):
            parts.append(lax.ppermute(parts[-1], "ka", core_ring))
        output_terms = dot_rows(jnp.concatenate(parts, axis=1), go)

        def output_chunk(dest):
            start = (((k - dest // per) % nk) * per + dest % per) * feat
            return lax.dynamic_slice(output_terms, (start, 0), (feat, width))

        live["g"] = jnp.zeros((2, nj, tok, 6 * feat), BF16)
        live["x"] = jnp.zeros((2 * nj * tok, width), BF16)
        keep("x", rows, 0, 0)
        come = {"r": [], "l": []}
        for step in range(1, nj + 1):
            for side in "rl":
                come[side].append(f"line{step}_{side}")
            if step < nj:
                part_r = output_chunk(jnp.minimum(nj - step + j, nj - 1))
                part_l = output_chunk(jnp.maximum(step + j - nj, 0))
                part_r = fill(jnp.where(j < step, part_r, 0.0))
                part_l = fill(jnp.where(j >= nj - step, part_l, 0.0))
                to_right = (live[f"line{step}_r"].astype(F32) + part_r).astype(BF16)
                to_left = (live[f"line{step}_l"].astype(F32) + part_l).astype(BF16)
                block = live[f"line{step}_l"]
                for near in range(1, step + 1):
                    block = jnp.where(j == nj - 1 - step + near, live[f"line{near}_r"], block)
                block = block[:tok]
                after = {1: ("dealt1",), 2: ("dealt3",), nj - 1: (f"swap{step}",)}
                if step < nj - 1:
                    along_z(f"line{step + 1}", to_right, to_left, after.get(step, ()))
                along_x(f"swap{step}", block, {2: ("swap0", "wk"), 3: ("wv",)}.get(step, ()))
                if step == nj - 1:
                    along_z(f"line{step + 1}", to_right, to_left, after[step])
                keep("x", block, step * tok, 0)
                if step > 1:
                    keep("x", live[f"swap{step - 1}"], (nj + step - 1) * tok, 0)
            if step == 1:
                for index in range(2, len(deals)):
                    deal(index)
            if step == 2:
                share(range(0, min(2, len(deals))))
        share(range(2, len(deals)))
        keep("x", live["swap0"], nj * tok, 0)
        w = jnp.concatenate(
            (query_weight, key_weight, value_weight, live["wq"], live["wk"], live["wv"]), axis=1
        )

        place = ring_place(j, nj)

        def chunk(bank, step):
            dest = ring_device((place - step) % nj, nj)
            part = lax.dynamic_index_in_dim(live["g"][bank], slot_of(dest), 0, keepdims=False)
            return dot_cols(part, w)

        def weight_term(w, count):
            part = live["g"].reshape(2 * nj * tok, 6 * feat)
            return dot_rows(live["x"], part[:, w * feat : (w + count) * feat])

        def hold(name):
            live["g"], live[name] = lax.optimization_barrier((live["g"], live[name]))

        other = chunk(1, 1).astype(BF16)
        own = lax.optimization_barrier(chunk(0, 1))
        (other,) = send("first", (f"swap{nj - 2}",), other1=other)
        live["other1"] = lax.ppermute(other, "ia", swap_x)
        hold(f"swap{nj - 1}")
        keep("x", live[f"swap{nj - 1}"], (2 * nj - 1) * tok, 0)
        along_y("pair", weight_term(3, 2).astype(BF16), ("other1",))
        for step in range(2, nj + 1):
            if step > 2:
                hold(f"other{step - 2}")
            after = {2: ("other1",), nj: ("pair",)}
            along_x(f"other{step}", chunk(1, step).astype(BF16), after.get(step, ()))
            term = own + live[f"other{step - 1}"].astype(F32)
            own = lax.optimization_barrier(chunk(0, step))
            if step > 2:
                term = lax.optimization_barrier(term) + live[f"sum{step - 2}"].astype(F32)
            (term,) = send("sum", **{f"sum{step - 1}": term.astype(BF16)})
            live[f"sum{step - 1}"] = lax.ppermute(term, "ja", ring)
        along_y("value", weight_term(5, 1).astype(BF16))
        grad_inputs = own + live[f"other{nj}"].astype(F32)
        grad_inputs = lax.optimization_barrier(grad_inputs) + live[f"sum{nj - 1}"].astype(F32)
        grad_inputs = grad_inputs.astype(BF16).reshape(inputs.shape)
        from_ends = live[f"line{nj}_r"].astype(F32) + live[f"line{nj}_l"].astype(F32)
        output_weight_grad = output_chunk(j) + from_ends[:feat]
        weight_grads = (
            weight_term(0, 1) + live["pair"][:, :feat].astype(F32),
            weight_term(1, 1) + live["pair"][:, feat:].astype(F32),
            weight_term(2, 1) + live["value"].astype(F32),
        )
        return (grad_inputs, *weight_grads, output_weight_grad)

    return local


def solution(mesh):
    return jax.shard_map(
        build(mesh),
        mesh=mesh,
        in_specs=(
            P("ia", "ja", "ka"),
            P(None, "ja", ("ia", "ka")),
            P("ia", "ja", "ka"),
            P(None, "ja", ("ia", "ka")),
            P(None, "ja", ("ia", "ka")),
            P(None, "ja", ("ia", "ka")),
            P("ka", ("ia", "ja")),
            P("ka", ("ia", "ja")),
            P("ka", ("ia", "ja")),
        ),
        out_specs=(
            P("ia", "ja", "ka"),
            P("ka", ("ia", "ja")),
            P("ka", ("ia", "ja")),
            P("ka", ("ia", "ja")),
            P(("ia", "ja"), "ka"),
        ),
        check_vma=False,
    )
```
